32 devices in a mesh: lat: 4 (over y, core), lon: 4 (over z), ens: 2 (over x).
Axes of the slice: x: 2, y: 2, z: 4, core: 2. Of those that a mesh axis runs over, the one named last changes fastest.
Arguments:
- fields: bfloat16 [2, 48, 64, 640], P('ens', 'lat', 'lon'), may hold values from -6 to 6
- filter_basis: bfloat16 [48, 5, 4, 16], P(('lat', 'lon')), may hold values from -0.625 to 0.625
- lon_offsets: int32 [48, 5, 16], P(('lat', 'lon')), may hold values from -32 to 31, as said below
- conv_weight: bfloat16 [2560, 640], replicated, may hold values from -0.125 to 0.125
- weight_in: bfloat16 [640, 1280], replicated, may hold values from -0.25 to 0.25
- weight_out: bfloat16 [1280, 640], replicated, may hold values from -0.15625 to 0.15625
- cotangent: bfloat16 [2, 48, 64, 640], P('ens', 'lat', 'lon'), may hold values from -6 to 6
Outputs:
- block_out: bfloat16 [2, 48, 64, 640], P('ens', 'lat', 'lon')
- field_grad: bfloat16 [2, 48, 64, 640], P('ens', 'lat', 'lon')
- conv_weight_grad: float32 [2560, 640], P(('lat', 'lon', 'ens'))
- weight_in_grad: float32 [640, 1280], P(None, ('lat', 'lon', 'ens'))
- weight_out_grad: float32 [1280, 640], P(('lat', 'lon', 'ens'))
The draws below stay inside these ranges and needn't reach their ends.
Inputs may be any that keep to these rules, and one draw needn't show every extreme that they name: `lon_offsets`: within one cycle and one cycle offset the 16 longitude offsets are distinct. In the 2 cycles nearest each pole they lie in -32 to 31; in every other cycle they lie in -16 to 15.
All inputs are finite; a program needn't handle non-finite values.
Results may differ from the reference program's by a relative error of at most 0.015.
Values may be sent and summed in bfloat16 or wider, within the bound.
A program may use at most 128 MiB of HBM per device.

```python
import math
import jax
import jax.numpy as jnp
from jax import lax

EMBED = 640
HIDDEN_SIZE = 1280
BASIS = 4
TAPS = 16
REACH_ROWS = 2
ROW_SPAN = 5
REACH_LON = 16
POLAR_CYCLES = 2
NLON = 64
NLAT = 48
MEMBERS = 2


def draw_lon_offsets(key, part):
    total_rows = NLAT * ROW_SPAN
    positions = jnp.arange(NLON, dtype=jnp.int32)
    scores = jax.random.randint(key, (total_rows, NLON), 0, 4096, dtype=jnp.int32) * NLON + positions[None, :]
    cycles = jnp.arange(total_rows, dtype=jnp.int32) // ROW_SPAN
    polar = (cycles < POLAR_CYCLES) | (cycles >= NLAT - POLAR_CYCLES)
    limits = jnp.where(polar, NLON, 2 * REACH_LON).astype(jnp.int32)
    scores = jnp.where(positions[None, :] < limits[:, None], scores, scores + 2 * 4096 * NLON)
    at_ends = (positions[None, :] == 0) | (positions[None, :] == NLON - 1)
    scores = jnp.where(polar[:, None] & at_ends, positions[None, :] - NLON, scores)
    ranked = jnp.argsort(scores, axis=1, stable=True).astype(jnp.int32)
    chosen = ranked[:, :TAPS] - (limits // 2)[:, None]
    return chosen.reshape(NLAT, ROW_SPAN, TAPS).astype(jnp.int32)


def levels(rng, extent, cuts, low, high):
    loudness = 1.0
    for position, shards_of in cuts:
        steps = jax.random.uniform(jax.random.fold_in(jax.random.fold_in(rng, 6), position), (shards_of,), jnp.float32, low / len(cuts), high / len(cuts))
        loudness = loudness * jnp.repeat(jnp.exp(steps), extent[position] // shards_of).reshape((-1,) + (1,) * (len(extent) - 1 - position))
    return loudness


def normal_values(own_key, dims, deviation, bound, shards=(), kind=jnp.bfloat16):
    level = levels(own_key, dims, shards, -0.22, 0.18) if shards else 1.0
    entries = jax.random.normal(own_key, dims, jnp.float32) * deviation * level
    return jnp.minimum(jnp.maximum(entries, -bound), bound).astype(kind)


def setup_inputs(seed: int = 0) -> dict:
    key_of = jax.random.split(jax.random.key(seed), 8)
    fields = normal_values(key_of[0], (MEMBERS, NLAT, NLON, EMBED), 1.0, 6.0, ((0, 2), (1, 4), (2, 4)))
    filter_basis = normal_values(key_of[1], (NLAT, ROW_SPAN, BASIS, TAPS), (ROW_SPAN * TAPS) ** -0.5, 0.625, ((0, 16),))
    lon_offsets = draw_lon_offsets(jax.random.fold_in(key_of[7], 71), 0)
    conv_weight = normal_values(key_of[3], (BASIS * EMBED, EMBED), (BASIS * EMBED) ** -0.5, 0.125)
    weight_in = normal_values(key_of[4], (EMBED, HIDDEN_SIZE), EMBED ** -0.5, 0.25)
    weight_out = normal_values(key_of[5], (HIDDEN_SIZE, EMBED), HIDDEN_SIZE ** -0.5, 0.15625)
    cotangent = normal_values(key_of[6], (MEMBERS, NLAT, NLON, EMBED), 1.0, 6.0, ((0, 2), (1, 4), (2, 4)))
    return dict(fields=fields, filter_basis=filter_basis, lon_offsets=lon_offsets, conv_weight=conv_weight, weight_in=weight_in, weight_out=weight_out, cotangent=cotangent)


half_root = 0.7071067811865476
gauss_norm = 0.3989422804014327

def feed_forward(blend_rows, tangent_rows, weight_in, weight_out):
    preact = jnp.dot(blend_rows, weight_in, preferred_element_type=jnp.float32)
    normal_cdf = 0.5 * (1.0 + jax.scipy.special.erf(preact * half_root))
    hidden_act = (preact * normal_cdf).astype(jnp.bfloat16)
    output_rows = (blend_rows.astype(jnp.float32) + jnp.dot(hidden_act, weight_out, preferred_element_type=jnp.float32)).astype(jnp.bfloat16)
    hidden_grad = lax.dot_general(tangent_rows, weight_out, (((1,), (1,)), ((), ())), preferred_element_type=jnp.float32)
    slope = normal_cdf + preact * jnp.exp(-0.5 * preact * preact) * gauss_norm
    preact_grad = (hidden_grad * slope).astype(jnp.bfloat16)
    blend_grad = (tangent_rows.astype(jnp.float32) + lax.dot_general(preact_grad, weight_in, (((1,), (1,)), ((), ())), preferred_element_type=jnp.float32)).astype(jnp.bfloat16)
    grad_in = lax.dot_general(blend_rows, preact_grad, (((0,), (0,)), ((), ())), preferred_element_type=jnp.float32)
    grad_out = lax.dot_general(hidden_act, tangent_rows, (((0,), (0,)), ((), ())), preferred_element_type=jnp.float32)
    return (output_rows, blend_grad, grad_in, grad_out)

def convolve(member_field, basis_float, lon_offsets):
    padded = jnp.pad(member_field, ((REACH_ROWS, REACH_ROWS), (0, 0), (0, 0)))
    columns = jnp.arange(NLON, dtype=jnp.int32)
    result = jnp.zeros((NLAT, NLON, BASIS, EMBED), member_field.dtype)
    for offset_row in range(ROW_SPAN):
        source = padded[offset_row:offset_row + NLAT]
        for tap_index in range(TAPS):
            lon_index = (columns[None, :] + lon_offsets[:, offset_row, tap_index][:, None]) % NLON
            shifted = jnp.take_along_axis(source, lon_index[:, :, None], axis=1)
            weights = basis_float[:, offset_row, :, tap_index]
            result = result + weights[:, None, :, None] * shifted[:, :, None, :]
    return result.reshape(NLAT, NLON, BASIS * EMBED)

def reference(fields, filter_basis, lon_offsets, conv_weight, weight_in, weight_out, cotangent):
    basis_float = filter_basis.astype(jnp.float32)

    def member(sums, inputs):
        member_field, tangent = inputs

        def local_conv(values):
            return convolve(values, basis_float, lon_offsets)
        spread_full, pullback = jax.vjp(local_conv, member_field.astype(jnp.float32))
        spread = spread_full.astype(jnp.bfloat16).reshape(NLAT * NLON, BASIS * EMBED)
        field_rows = member_field.reshape(NLAT * NLON, EMBED)
        blended = (field_rows.astype(jnp.float32) + jnp.dot(spread, conv_weight, preferred_element_type=jnp.float32)).astype(jnp.bfloat16)
        tangent_rows = tangent.reshape(NLAT * NLON, EMBED)
        output_rows, blend_grad, grad_in, grad_out = feed_forward(blended, tangent_rows, weight_in, weight_out)
        spread_grad = lax.dot_general(blend_grad, conv_weight, (((1,), (1,)), ((), ())), preferred_element_type=jnp.float32).astype(jnp.bfloat16)
        adjoint, = pullback(spread_grad.astype(jnp.float32).reshape(NLAT, NLON, BASIS * EMBED))
        member_grad = (blend_grad.astype(jnp.float32).reshape(NLAT, NLON, EMBED) + adjoint).astype(jnp.bfloat16)
        grad_conv = lax.dot_general(spread, blend_grad, (((0,), (0,)), ((), ())), preferred_element_type=jnp.float32)
        new_sums = (sums[0] + grad_conv, sums[1] + grad_in, sums[2] + grad_out)
        return (new_sums, (output_rows.reshape(NLAT, NLON, EMBED), member_grad))
    start_sums = (jnp.zeros((BASIS * EMBED, EMBED), jnp.float32), jnp.zeros((EMBED, HIDDEN_SIZE), jnp.float32), jnp.zeros((HIDDEN_SIZE, EMBED), jnp.float32))
    sums, (block_out, field_grad) = lax.scan(member, start_sums, (fields, cotangent))
    factor = 1.0 / math.sqrt(MEMBERS * NLAT * NLON)
    return (block_out, field_grad, sums[0] * factor, sums[1] * factor, sums[2] * factor)
```

```python
import functools
import math

import jax
import jax.numpy as jnp
from jax import lax
from jax.experimental import pallas as pl
from jax.experimental.pallas import tpu as pltpu
from jax.sharding import PartitionSpec as P

HALF_ROOT = 0.7071067811865476
GAUSS_NORM = 0.3989422804014327
MESH = pl.DeviceIdType.MESH
F32 = jnp.float32
BF16 = jnp.bfloat16


def mm(left, right, contract):
    return lax.dot_general(left, right, ((contract[:1], contract[1:]), ((), ())),
                           preferred_element_type=F32)


class Plan:
    def __init__(self, fields, filter_basis, weight_in):
        self.lat, self.lon = lax.axis_size("lat"), lax.axis_size("lon")
        self.ens = lax.axis_size("ens")
        _, self.tile, self.width, self.embed = fields.shape
        self.band, self.span, self.basis, self.taps = filter_basis.shape
        self.hidden = weight_in.shape[1]
        self.reach = self.span // 2
        self.nlon = self.lon * self.width
        self.cells = self.band * self.nlon
        self.cores = 2 if self.lat % 2 == 0 else 1
        self.rows = self.lat // self.cores
        self.members = 1
        for members in (self.ens, 1):
            blocks = self.lat * self.lon * members
            conv_rows = self.basis * self.embed // blocks
            in_rows = self.hidden // blocks
            if conv_rows % 16 == 0 and in_rows % 8 == 0 and self.embed % conv_rows == 0:
                self.members = members
                break
        self.blocks = self.lat * self.lon * self.members
        self.conv_rows = self.basis * self.embed // self.blocks
        self.in_rows = self.hidden // self.blocks
        self.half = self.blocks // self.cores


def kernel(
    g, taps_ref, fields, cot, conv_hbm, in_hbm, out_hbm,
    block_out, field_grad, conv_out, io_out,
    conv_w, w_in, w_out, win, cot_band, matrix, spread, blended, hidden, pgrad, bgrad,
    sgrad, adj, bo_band, fg_band, rim_send, rim_recv,
    conv_g, io_g, conv_c, io_c, conv_s0, io_s0, conv_r1, io_r1, conv_s1, io_s1,
    conv_r2, io_r2, conv_s2, io_s2, conv_r3, io_r3,
    local_sem, gather_send, gather_recv, edge_sem, cot_send, cot_recv,
    bo_send, bo_recv, fg_send, fg_recv, rim_ssem, rim_rsem,
    core_send, core_recv, st_send, st_recv,
):
    a, j, e = lax.axis_index("lat"), lax.axis_index("lon"), lax.axis_index("ens")
    L, s, W, T, C = g.lon, g.band, g.width, g.tile, g.embed
    rr = g.reach
    core, y = lax.rem(a, g.cores), lax.div(a, g.cores)
    b = a * L + j
    last = g.lat * L - 1

    def remote(src, dst, ssem, rsem, **device):
        return pltpu.make_async_remote_copy(
            src_ref=src, dst_ref=dst, send_sem=ssem, recv_sem=rsem,
            device_id=device, device_id_type=MESH)

    def columns(index):
        return pl.ds(pl.multiple_of(index * W, W), W)

    weights = [
        pltpu.make_async_copy(src, dst, local_sem.at[i])
        for i, (src, dst) in enumerate(((conv_hbm, conv_w), (in_hbm, w_in), (out_hbm, w_out)))
    ]
    own_field = pltpu.make_async_copy(
        fields.at[0, pl.ds(j * s, s)], win.at[pl.ds(rr, s), columns(j)], local_sem.at[3])
    own_cot = pltpu.make_async_copy(
        cot.at[0, pl.ds(j * s, s)], cot_band.at[:, columns(j)], local_sem.at[4])
    own_field.start()
    own_cot.start()

    barrier = pltpu.get_barrier_semaphore()
    count = 0
    for step in (1, g.lat - 1):
        for q in range(L):
            pl.semaphore_signal(barrier, inc=1, device_id_type=MESH,
                                device_id={"lat": lax.rem(a + step, g.lat), "lon": q})
            count += 1
    for d in range(1, L):
        pl.semaphore_signal(barrier, inc=1, device_id_type=MESH,
                            device_id={"lon": lax.rem(j + d, L)})
        count += 1
    for d in range(1, g.rows):
        pl.semaphore_signal(barrier, inc=1, device_id_type=MESH,
                            device_id={"lat": lax.rem(y + d, g.rows) * g.cores + core})
        count += 1
    for d in range(1, g.members):
        pl.semaphore_signal(barrier, inc=1, device_id_type=MESH,
                            device_id={"ens": lax.rem(e + d, g.members)})
        count += 1
    pl.semaphore_wait(barrier, count)

    def low_src(p):
        return fields.at[0, pl.ds(lax.rem(p * s - rr + T, T), rr)]

    def high_src(p):
        return fields.at[0, pl.ds(lax.rem(p * s + s, T), rr)]

    low_rows, mid_rows, high_rows = pl.ds(0, rr), pl.ds(rr, s), pl.ds(rr + s, rr)

    def up(p):
        return lax.rem(a + (p == 0).astype(jnp.int32), g.lat)

    def down(p):
        return lax.rem(a + g.lat - (p == L - 1).astype(jnp.int32), g.lat)

    sends = []
    for d in range(1, L):
        p = lax.rem(j + d, L)
        triple = (
            (fields.at[0, pl.ds(p * s, s)], mid_rows, a),
            (low_src(p), low_rows, up(p)),
            (high_src(p), high_rows, down(p)),
        )
        for i, (src, rows, row) in enumerate(triple):
            copy = remote(src, win.at[rows, columns(j)], gather_send.at[d - 1, i],
                          gather_recv.at[d - 1, i], lat=row, lon=p)
            copy.start()
            sends.append(copy)
    low_local = pltpu.make_async_copy(low_src(j), win.at[low_rows, columns(j)], edge_sem.at[0])
    low_remote = remote(low_src(j), win.at[low_rows, columns(j)], edge_sem.at[2],
                        edge_sem.at[0], lat=lax.rem(a + 1, g.lat))
    high_local = pltpu.make_async_copy(high_src(j), win.at[high_rows, columns(j)], edge_sem.at[1])
    high_remote = remote(high_src(j), win.at[high_rows, columns(j)], edge_sem.at[3],
                         edge_sem.at[1], lat=lax.rem(a + g.lat - 1, g.lat))

    @pl.when(j == 0)
    def _():
        low_remote.start()

    @pl.when(j != 0)
    def _():
        low_local.start()

    @pl.when(j == L - 1)
    def _():
        high_remote.start()

    @pl.when(j != L - 1)
    def _():
        high_local.start()

    for d in range(1, L):
        p = lax.rem(j + d, L)
        copy = remote(cot.at[0, pl.ds(p * s, s)], cot_band.at[:, columns(j)],
                      cot_send.at[d - 1], cot_recv.at[d - 1], lon=p)
        copy.start()
        sends.append(copy)
    for copy in weights:
        copy.start()

    NL, K, TAPS = g.nlon, g.basis, g.taps
    wide = g.span * NL
    step_rows = 16
    steps = NL // step_rows
    places = lax.broadcasted_iota(jnp.int32, (step_rows, wide), 1)
    lines = lax.broadcasted_iota(jnp.int32, (step_rows, wide), 0)

    def build(i, _):
        r, n0 = lax.div(i, steps), lax.rem(i, steps) * step_rows
        gap = lax.rem(lax.rem(places, NL) - lines - n0 + (NL + NL // 2), NL) - NL // 2
        gap = gap.astype(F32)
        sums = [jnp.zeros((step_rows, wide), F32) for _ in range(K)]
        for t in range(TAPS):
            hit = gap == taps_ref[r, pl.ds(t, 1), :]
            for k in range(K):
                value = taps_ref[r, pl.ds(TAPS * (k + 1) + t, 1), :]
                sums[k] = jnp.where(hit, value, sums[k])
        for k in range(K):
            start = pl.multiple_of(k * NL + n0, step_rows)
            matrix[r, pl.ds(start, step_rows), :] = sums[k].astype(BF16)
        return 0

    lax.fori_loop(0, s * steps, build, 0)

    own_field.wait()
    for d in range(1, L):
        source = lax.rem(j - d + L, L)
        for i, rows in enumerate((mid_rows, low_rows, high_rows)):
            landed = win.at[rows, columns(source)]
            remote(landed, landed, gather_send.at[d - 1, i], gather_recv.at[d - 1, i],
                   lon=source).wait_recv()

    @pl.when(j == 0)
    def _():
        low_remote.wait()

    @pl.when(j != 0)
    def _():
        low_local.wait()

    @pl.when(j == L - 1)
    def _():
        high_remote.wait()

    @pl.when(j != L - 1)
    def _():
        high_local.wait()

    @pl.when(b == 0)
    def _():
        win[0:rr] = jnp.zeros((rr, NL, C), BF16)

    @pl.when(b == last)
    def _():
        win[rr + s:] = jnp.zeros((rr, NL, C), BF16)

    for r in range(s):
        window = win[r:r + g.span].reshape(wide, C)
        part = mm(matrix[r], window, (1, 0)).astype(BF16)
        for k in range(K):
            spread[r * NL:(r + 1) * NL, k * C:(k + 1) * C] = part[k * NL:(k + 1) * NL]
    weights[0].wait()
    blended[...] = (
        win[rr:rr + s].reshape(g.cells, C).astype(F32) + mm(spread[...], conv_w[...], (1, 0))
    ).astype(BF16)

    own_cot.wait()
    for d in range(1, L):
        source = lax.rem(j - d + L, L)
        landed = cot_band.at[:, columns(source)]
        remote(landed, landed, cot_send.at[d - 1], cot_recv.at[d - 1], lon=source).wait_recv()
    weights[1].wait()
    weights[2].wait()
    lanes = 256 if g.hidden % 256 == 0 else g.hidden

    def units(i, _):
        cols = pl.ds(pl.multiple_of(i * lanes, lanes), lanes)
        pre = mm(blended[...], w_in[:, cols], (1, 0))
        cdf = 0.5 * (1.0 + lax.erf(pre * HALF_ROOT))
        hidden[:, cols] = (pre * cdf).astype(BF16)
        hgrad = mm(cot_band[...].reshape(g.cells, C), w_out[cols, :], (1, 1))
        slope = cdf + pre * jnp.exp(-0.5 * pre * pre) * GAUSS_NORM
        pgrad[:, cols] = (hgrad * slope).astype(BF16)
        return 0

    lax.fori_loop(0, g.hidden // lanes, units, 0)

    def send_tiles(band, out, ssem, rsem):
        copies = []
        for d in range(1, L):
            p = lax.rem(j + d, L)
            copy = remote(band.at[:, columns(p)], out.at[0, pl.ds(j * s, s)],
                          ssem.at[d - 1], rsem.at[d - 1], lon=p)
            copy.start()
            copies.append(copy)
        out[0, pl.ds(j * s, s)] = band[:, columns(j), :]
        return copies

    def await_tiles(out, ssem, rsem):
        for d in range(1, L):
            source = lax.rem(j - d + L, L)
            landed = out.at[0, pl.ds(source * s, s)]
            remote(landed, landed, ssem.at[d - 1], rsem.at[d - 1], lon=source).wait_recv()

    E, Y, half = g.members, g.rows, g.half
    ri, rc = g.in_rows, g.conv_rows

    def place(index, order):
        member = lax.rem(index, E)
        column = lax.rem(lax.div(index, E), L)
        row = lax.div(index, E * L)
        row_core, row_y = lax.rem(row, g.cores), lax.div(row, g.cores)
        if order == "ens":
            return row_core, (member * Y + row_y) * L + column
        return row_core, (row_y * E + member) * L + column

    def io_blocks(i, _):
        cols = pl.ds(pl.multiple_of(i * C, 128), C)
        left = mm(pgrad[:, cols], blended[...], (0, 0))
        right = mm(hidden[:, cols], cot_band[...].reshape(g.cells, C), (0, 0))
        for c in range(C // ri):
            where, flat = place(i * (C // ri) + c, "ens")
            both = jnp.concatenate([left[c * ri:(c + 1) * ri], right[c * ri:(c + 1) * ri]], 0)
            io_g[where, flat] = both.astype(BF16)
        return 0

    lax.fori_loop(0, g.hidden // C, io_blocks, 0)

    def core_copy(src, dst, index):
        return remote(src.at[1 - core], dst, core_send.at[index], core_recv.at[index],
                      lat=y * g.cores + 1 - core)

    io_core = core_copy(io_g, io_c, 0)
    conv_core = core_copy(conv_g, conv_c, 1)
    if g.cores > 1:
        io_core.start()

    bo_band[...] = (
        blended[...].astype(F32) + mm(hidden[...], w_out[...], (1, 0))
    ).astype(BF16).reshape(s, NL, C)
    sends += send_tiles(bo_band, block_out, bo_send, bo_recv)
    bgrad[...] = (
        cot_band[...].reshape(g.cells, C).astype(F32) + mm(pgrad[...], w_in[...], (1, 1))
    ).astype(BF16)

    def core_sum(total, own, other):
        def one(i, _):
            block = own[core, i].astype(F32)
            if g.cores > 1:
                block = block + other[i].astype(F32)
            total[i] = block.astype(BF16)
            return 0
        lax.fori_loop(0, half, one, 0)

    def peer(axis, d):
        if axis == "ens":
            return E, e, {"ens": lax.rem(e + d, E)}, lax.rem(e + d, E)
        if axis == "lat":
            p = lax.rem(y + d, Y)
            return Y, y, {"lat": p * g.cores + core}, p
        p = lax.rem(j + d, L)
        return L, j, {"lon": p}, p

    def sizes(axis):
        return {"ens": E, "lat": Y, "lon": L}[axis]

    def stage_start(axis, src, dst, sem_row):
        n = sizes(axis)
        m = src.shape[0] // n
        copies = []
        for d in range(1, n):
            _, _, device, p = peer(axis, d)
            copy = remote(src.at[pl.ds(p * m, m)], dst.at[d - 1],
                          st_send.at[sem_row, d - 1], st_recv.at[sem_row, d - 1], **device)
            copy.start()
            copies.append(copy)
        return copies

    def stage_sum(axis, src, dst, total, copies, scale=None):
        n = sizes(axis)
        m = src.shape[0] // n
        me = peer(axis, 0)[1]
        for copy in copies:
            copy.wait()

        def one(i, _):
            block = src[me * m + i].astype(F32)
            for d in range(1, n):
                block = block + dst[d - 1, i].astype(F32)
            if total.dtype == BF16:
                total[i] = block.astype(BF16)
            else:
                total[...] = block
            return 0

        lax.fori_loop(0, m, one, 0)

    if g.cores > 1:
        io_core.wait()
    core_sum(io_s0, io_g, io_c)
    io_1 = stage_start("ens", io_s0, io_r1, 0)

    sgrad[...] = mm(bgrad[...], conv_w[...], (1, 1)).astype(BF16)
    for r in range(s):
        grad = jnp.concatenate(
            [sgrad[r * NL:(r + 1) * NL, k * C:(k + 1) * C] for k in range(K)], 0)
        part = mm(matrix[r], grad, (0, 0)).reshape(g.span, NL, C)
        if r == 0:
            adj[0:g.span] = part
            adj[g.span:] = jnp.zeros((s - 1, NL, C), F32)
        else:
            adj[r:r + g.span] += part

    rim_send[0] = adj[0:rr].astype(BF16)
    rim_send[1] = adj[rr + s:].astype(BF16)
    before = lax.rem(b + last, last + 1)
    after = lax.rem(b + 1, last + 1)
    rims = [
        remote(rim_send.at[0], rim_recv.at[0], rim_ssem.at[0], rim_rsem.at[0],
               lat=lax.div(before, L), lon=lax.rem(before, L)),
        remote(rim_send.at[1], rim_recv.at[1], rim_ssem.at[1], rim_rsem.at[1],
               lat=lax.div(after, L), lon=lax.rem(after, L)),
    ]
    for copy in rims:
        copy.start()

    def conv_blocks(i, _):
        cols = pl.ds(pl.multiple_of(i * C, 128), C)
        product = mm(spread[:, cols], bgrad[...], (0, 0))
        for c in range(C // rc):
            where, flat = place(i * (C // rc) + c, "lat")
            conv_g[where, flat] = product[c * rc:(c + 1) * rc].astype(BF16)
        return 0

    lax.fori_loop(0, K, conv_blocks, 0)
    if g.cores > 1:
        conv_core.start()

    for copy in rims:
        copy.wait()
    from_next = jnp.where(b == last, 0.0, rim_recv[0].astype(F32))
    from_prev = jnp.where(b == 0, 0.0, rim_recv[1].astype(F32))
    adj[rr:2 * rr] += from_prev
    adj[s:s + rr] += from_next
    fg_band[...] = (
        bgrad[...].astype(F32).reshape(s, NL, C) + adj[rr:rr + s]
    ).astype(BF16)
    sends += send_tiles(fg_band, field_grad, fg_send, fg_recv)

    if g.cores > 1:
        conv_core.wait()
    core_sum(conv_s0, conv_g, conv_c)
    conv_1 = stage_start("lat", conv_s0, conv_r1, 1)
    stage_sum("ens", io_s0, io_r1, io_s1, io_1)
    io_2 = stage_start("lat", io_s1, io_r2, 2)
    stage_sum("lat", conv_s0, conv_r1, conv_s1, conv_1)
    conv_2 = stage_start("ens", conv_s1, conv_r2, 3)
    stage_sum("lat", io_s1, io_r2, io_s2, io_2)
    io_3 = stage_start("lon", io_s2, io_r3, 4)
    stage_sum("ens", conv_s1, conv_r2, conv_s2, conv_2)
    conv_3 = stage_start("lon", conv_s2, conv_r3, 5)
    await_tiles(block_out, bo_send, bo_recv)
    await_tiles(field_grad, fg_send, fg_recv)
    stage_sum("lon", io_s2, io_r3, io_out, io_3)
    stage_sum("lon", conv_s2, conv_r3, conv_out, conv_3)
    for copy in sends:
        copy.wait_send()


def shards(fields, filter_basis, lon_offsets, conv_weight, weight_in, weight_out, cotangent):
    g = Plan(fields, filter_basis, weight_in)
    C, H, K, L, s = g.embed, g.hidden, g.basis, g.lon, g.band
    table = jnp.concatenate(
        [lon_offsets.astype(F32)[:, :, None, :], filter_basis.astype(F32)], axis=2)
    table = table.transpose(0, 2, 3, 1).reshape(s, (K + 1) * g.taps, g.span)
    table = jnp.repeat(table, g.nlon, axis=2)

    vmem, dma = pltpu.VMEM, pltpu.SemaphoreType.DMA
    rc, rio, half = g.conv_rows, 2 * g.in_rows, g.half
    peers = max(L, g.rows, g.members, 2) - 1

    def slots(n):
        return max(n - 1, 1)

    after_ens, after_lat = half // g.members, half // g.rows
    scratch = [
        vmem((K * C, C), BF16), vmem((C, H), BF16), vmem((H, C), BF16),
        vmem((s + 2 * g.reach, g.nlon, C), BF16), vmem((s, g.nlon, C), BF16),
        vmem((s, K * g.nlon, g.span * g.nlon), BF16), vmem((g.cells, K * C), BF16),
        vmem((g.cells, C), BF16), vmem((g.cells, H), BF16), vmem((g.cells, H), BF16),
        vmem((g.cells, C), BF16), vmem((g.cells, K * C), BF16),
        vmem((s + 2 * g.reach, g.nlon, C), F32),
        vmem((s, g.nlon, C), BF16), vmem((s, g.nlon, C), BF16),
        vmem((2, g.reach, g.nlon, C), BF16), vmem((2, g.reach, g.nlon, C), BF16),
        vmem((g.cores, half, rc, C), BF16), vmem((g.cores, half, rio, C), BF16),
        vmem((half, rc, C), BF16), vmem((half, rio, C), BF16),
        vmem((half, rc, C), BF16), vmem((half, rio, C), BF16),
        vmem((slots(g.rows), after_lat, rc, C), BF16),
        vmem((slots(g.members), after_ens, rio, C), BF16),
        vmem((after_lat, rc, C), BF16), vmem((after_ens, rio, C), BF16),
        vmem((slots(g.members), L, rc, C), BF16), vmem((slots(g.rows), L, rio, C), BF16),
        vmem((L, rc, C), BF16), vmem((L, rio, C), BF16),
        vmem((slots(L), 1, rc, C), BF16), vmem((slots(L), 1, rio, C), BF16),
        dma((5,)), dma((slots(L), 3)), dma((slots(L), 3)), dma((4,)),
        dma((slots(L),)), dma((slots(L),)), dma((slots(L),)), dma((slots(L),)),
        dma((slots(L),)), dma((slots(L),)), dma((2,)), dma((2,)),
        dma((2,)), dma((2,)), dma((6, peers)), dma((6, peers)),
    ]
    in_vmem = pl.BlockSpec(memory_space=pltpu.VMEM)
    anywhere = pl.BlockSpec(memory_space=pl.ANY)
    block_out, field_grad, conv_sum, io_sum = pl.pallas_call(
        functools.partial(kernel, g),
        out_shape=(
            jax.ShapeDtypeStruct(fields.shape, BF16),
            jax.ShapeDtypeStruct(fields.shape, BF16),
            jax.ShapeDtypeStruct((rc, C), F32),
            jax.ShapeDtypeStruct((rio, C), F32),
        ),
        in_specs=[in_vmem] + [anywhere] * 5,
        out_specs=(in_vmem,) * 4,
        scratch_shapes=scratch,
        compiler_params=pltpu.CompilerParams(
            collective_id=0, has_side_effects=True, vmem_limit_bytes=56 * 1024 * 1024),
        cost_estimate=pl.CostEstimate(
            flops=24 * g.cells * C * H, bytes_accessed=16 * C * H, transcendentals=2 * g.cells * H),
    )(table, fields, cotangent, conv_weight, weight_in, weight_out)

    in_sum, out_sum = io_sum[:g.in_rows], io_sum[g.in_rows:]
    if g.members < g.ens:
        conv_sum, in_sum, out_sum = (
            lax.psum_scatter(part.astype(BF16), "ens", scatter_dimension=0, tiled=True).astype(F32)
            for part in (conv_sum, in_sum, out_sum)
        )
    factor = 1.0 / math.sqrt(g.ens * g.lat * L * g.cells)
    return (block_out, field_grad, conv_sum * factor, in_sum.T * factor, out_sum * factor)


def solution(mesh):
    tiles = P("ens", "lat", "lon", None)
    bands = ("lat", "lon")
    blocks = ("lat", "lon", "ens")
    return jax.shard_map(
        shards,
        mesh=mesh,
        in_specs=(tiles, P(bands, None, None, None), P(bands, None, None), P(), P(), P(), tiles),
        out_specs=(tiles, tiles, P(blocks, None), P(None, blocks), P(blocks, None)),
        check_vma=False,
    )
```

```python
import functools
import math

import jax
import jax.numpy as jnp
from jax import lax
from jax.experimental import pallas as pl
from jax.experimental.pallas import tpu as pltpu
from jax.sharding import PartitionSpec as P

HALF_ROOT = 0.7071067811865476
GAUSS_NORM = 0.3989422804014327
MESH = pl.DeviceIdType.MESH
F32 = jnp.float32
BF16 = jnp.bfloat16


def mm(left, right, contract):
    return lax.dot_general(left, right, ((contract[:1], contract[1:]), ((), ())),
                           preferred_element_type=F32)


class Plan:
    def __init__(self, fields, filter_basis, weight_in):
        self.lat, self.lon = lax.axis_size("lat"), lax.axis_size("lon")
        self.ens = lax.axis_size("ens")
        _, self.tile, self.width, self.embed = fields.shape
        self.band, self.span, self.basis, self.taps = filter_basis.shape
        self.hidden = weight_in.shape[1]
        self.reach = self.span // 2
        self.nlon = self.lon * self.width
        self.cells = self.band * self.nlon
        self.cores = 2 if self.lat % 2 == 0 else 1
        self.rows = self.lat // self.cores
        self.members = 1
        for members in (self.ens, 1):
            blocks = self.lat * self.lon * members
            conv_rows = self.basis * self.embed // blocks
            in_rows = self.hidden // blocks
            if conv_rows % 16 == 0 and in_rows % 8 == 0 and self.embed % conv_rows == 0:
                self.members = members
                break
        self.blocks = self.lat * self.lon * self.members
        self.conv_rows = self.basis * self.embed // self.blocks
        self.in_rows = self.hidden // self.blocks
        self.half = self.blocks // self.cores
        order = sorted(range(self.lon), key=lambda q: (-abs(2 * q - self.lon + 1), q))
        self.groups = 2 if self.lon % 2 == 0 else 1
        self.group_size = self.lon // self.groups
        self.spot = [order.index(q) for q in range(self.lon)]


def kernel(
    g, taps_hbm, fields, cot, conv_hbm, in_hbm, out_hbm,
    block_out, field_grad, conv_out, io_out,
    taps_ref, conv_w, w_in, w_out, win, cot_band, matrix, spread, blended, hidden, pgrad, bgrad,
    sgrad, adj, bo_band, fg_band, rim_send, rim_recv,
    conv_g, io_g, conv_c, io_c, conv_s0, io_s0, conv_r1, io_r1, conv_s1, io_s1,
    conv_r2, io_r2, conv_s2, io_s2, conv_r3, io_r3,
    local_sem, gather_send, gather_recv, edge_sem, cot_send, cot_recv,
    bo_send, bo_recv, fg_send, fg_recv, rim_ssem, rim_rsem,
    core_send, core_recv, st_send, st_recv, lon_send, lon_recv,
):
    a, j, e = lax.axis_index("lat"), lax.axis_index("lon"), lax.axis_index("ens")
    L, s, W, T, C = g.lon, g.band, g.width, g.tile, g.embed
    rr = g.reach
    core, y = lax.rem(a, g.cores), lax.div(a, g.cores)
    b = a * L + j
    last = g.lat * L - 1

    def remote(src, dst, ssem, rsem, **device):
        return pltpu.make_async_remote_copy(
            src_ref=src, dst_ref=dst, send_sem=ssem, recv_sem=rsem,
            device_id=device, device_id_type=MESH)

    def columns(index):
        return pl.ds(pl.multiple_of(index * W, W), W)

    weights = [
        pltpu.make_async_copy(src, dst, local_sem.at[i])
        for i, (src, dst) in enumerate(((conv_hbm, conv_w), (in_hbm, w_in), (out_hbm, w_out)))
    ]
    own_field = pltpu.make_async_copy(
        fields.at[0, pl.ds(j * s, s)], win.at[pl.ds(rr, s), columns(j)], local_sem.at[3])
    own_cot = pltpu.make_async_copy(
        cot.at[0, pl.ds(j * s, s)], cot_band.at[:, columns(j)], local_sem.at[4])
    table = pltpu.make_async_copy(taps_hbm, taps_ref, local_sem.at[5])
    table.start()
    own_field.start()
    own_cot.start()

    barrier = pltpu.get_barrier_semaphore()
    count = 0
    for step in (1, g.lat - 1):
        for q in range(L):
            pl.semaphore_signal(barrier, inc=1, device_id_type=MESH,
                                device_id={"lat": lax.rem(a + step, g.lat), "lon": q})
            count += 1
    for d in range(1, L):
        pl.semaphore_signal(barrier, inc=1, device_id_type=MESH,
                            device_id={"lon": lax.rem(j + d, L)})
        count += 1
    for d in range(1, g.rows):
        pl.semaphore_signal(barrier, inc=1, device_id_type=MESH,
                            device_id={"lat": lax.rem(y + d, g.rows) * g.cores + core})
        count += 1
    for d in range(1, g.members):
        pl.semaphore_signal(barrier, inc=1, device_id_type=MESH,
                            device_id={"ens": lax.rem(e + d, g.members)})
        count += 1
    pl.semaphore_wait(barrier, count)

    def low_src(p):
        return fields.at[0, pl.ds(lax.rem(p * s - rr + T, T), rr)]

    def high_src(p):
        return fields.at[0, pl.ds(lax.rem(p * s + s, T), rr)]

    low_rows, mid_rows, high_rows = pl.ds(0, rr), pl.ds(rr, s), pl.ds(rr + s, rr)

    def up(p):
        return lax.rem(a + (p == 0).astype(jnp.int32), g.lat)

    def down(p):
        return lax.rem(a + g.lat - (p == L - 1).astype(jnp.int32), g.lat)

    sends = []
    for d in range(1, L):
        p = lax.rem(j + d, L)
        triple = (
            (fields.at[0, pl.ds(p * s, s)], mid_rows, a),
            (low_src(p), low_rows, up(p)),
            (high_src(p), high_rows, down(p)),
        )
        for i, (src, rows, row) in enumerate(triple):
            copy = remote(src, win.at[rows, columns(j)], gather_send.at[d - 1, i],
                          gather_recv.at[d - 1, i], lat=row, lon=p)
            copy.start()
            sends.append(copy)
    low_local = pltpu.make_async_copy(low_src(j), win.at[low_rows, columns(j)], edge_sem.at[0])
    low_remote = remote(low_src(j), win.at[low_rows, columns(j)], edge_sem.at[2],
                        edge_sem.at[0], lat=lax.rem(a + 1, g.lat))
    high_local = pltpu.make_async_copy(high_src(j), win.at[high_rows, columns(j)], edge_sem.at[1])
    high_remote = remote(high_src(j), win.at[high_rows, columns(j)], edge_sem.at[3],
                         edge_sem.at[1], lat=lax.rem(a + g.lat - 1, g.lat))

    @pl.when(j == 0)
    def _():
        low_remote.start()

    @pl.when(j != 0)
    def _():
        low_local.start()

    @pl.when(j == L - 1)
    def _():
        high_remote.start()

    @pl.when(j != L - 1)
    def _():
        high_local.start()

    for d in range(1, L):
        p = lax.rem(j + d, L)
        copy = remote(cot.at[0, pl.ds(p * s, s)], cot_band.at[:, columns(j)],
                      cot_send.at[d - 1], cot_recv.at[d - 1], lon=p)
        copy.start()
        sends.append(copy)
    for copy in weights:
        copy.start()

    NL, K, TAPS = g.nlon, g.basis, g.taps
    wide = g.span * NL
    step_rows = 16
    steps = NL // step_rows
    places = lax.broadcasted_iota(jnp.int32, (step_rows, wide), 1)
    lines = lax.broadcasted_iota(jnp.int32, (step_rows, wide), 0)

    def build(i, _):
        r, n0 = lax.div(i, steps), lax.rem(i, steps) * step_rows
        gap = lax.rem(lax.rem(places, NL) - lines - n0 + (NL + NL // 2), NL) - NL // 2
        gap = gap.astype(F32)
        sums = [jnp.zeros((step_rows, wide), F32) for _ in range(K)]
        for t in range(TAPS):
            hit = gap == taps_ref[r, pl.ds(t, 1), :]
            for k in range(K):
                value = taps_ref[r, pl.ds(TAPS * (k + 1) + t, 1), :]
                sums[k] = jnp.where(hit, value, sums[k])
        for k in range(K):
            start = pl.multiple_of(k * NL + n0, step_rows)
            matrix[r, pl.ds(start, step_rows), :] = sums[k].astype(BF16)
        return 0

    table.wait()
    lax.fori_loop(0, s * steps, build, 0)

    own_field.wait()
    for d in range(1, L):
        source = lax.rem(j - d + L, L)
        for i, rows in enumerate((mid_rows, low_rows, high_rows)):
            landed = win.at[rows, columns(source)]
            remote(landed, landed, gather_send.at[d - 1, i], gather_recv.at[d - 1, i],
                   lon=source).wait_recv()

    @pl.when(j == 0)
    def _():
        low_remote.wait()

    @pl.when(j != 0)
    def _():
        low_local.wait()

    @pl.when(j == L - 1)
    def _():
        high_remote.wait()

    @pl.when(j != L - 1)
    def _():
        high_local.wait()

    @pl.when(b == 0)
    def _():
        win[0:rr] = jnp.zeros((rr, NL, C), BF16)

    @pl.when(b == last)
    def _():
        win[rr + s:] = jnp.zeros((rr, NL, C), BF16)

    for r in range(s):
        window = win[r:r + g.span].reshape(wide, C)
        part = mm(matrix[r], window, (1, 0)).astype(BF16)
        for k in range(K):
            spread[r * NL:(r + 1) * NL, k * C:(k + 1) * C] = part[k * NL:(k + 1) * NL]
    weights[0].wait()
    blended[...] = (
        win[rr:rr + s].reshape(g.cells, C).astype(F32) + mm(spread[...], conv_w[...], (1, 0))
    ).astype(BF16)

    own_cot.wait()
    for d in range(1, L):
        source = lax.rem(j - d + L, L)
        landed = cot_band.at[:, columns(source)]
        remote(landed, landed, cot_send.at[d - 1], cot_recv.at[d - 1], lon=source).wait_recv()
    weights[1].wait()
    weights[2].wait()
    lanes = 256 if g.hidden % 256 == 0 else g.hidden

    def units(i, _):
        cols = pl.ds(pl.multiple_of(i * lanes, lanes), lanes)
        pre = mm(blended[...], w_in[:, cols], (1, 0))
        cdf = 0.5 * (1.0 + lax.erf(pre * HALF_ROOT))
        hidden[:, cols] = (pre * cdf).astype(BF16)
        hgrad = mm(cot_band[...].reshape(g.cells, C), w_out[cols, :], (1, 1))
        slope = cdf + pre * jnp.exp(-0.5 * pre * pre) * GAUSS_NORM
        pgrad[:, cols] = (hgrad * slope).astype(BF16)
        return 0

    lax.fori_loop(0, g.hidden // lanes, units, 0)

    def send_tiles(band, out, ssem, rsem):
        copies = []
        for d in range(1, L):
            p = lax.rem(j + d, L)
            copy = remote(band.at[:, columns(p)], out.at[0, pl.ds(j * s, s)],
                          ssem.at[d - 1], rsem.at[d - 1], lon=p)
            copy.start()
            copies.append(copy)
        out[0, pl.ds(j * s, s)] = band[:, columns(j), :]
        return copies

    def await_tiles(out, ssem, rsem):
        for d in range(1, L):
            source = lax.rem(j - d + L, L)
            landed = out.at[0, pl.ds(source * s, s)]
            remote(landed, landed, ssem.at[d - 1], rsem.at[d - 1], lon=source).wait_recv()

    E, Y, half = g.members, g.rows, g.half
    ri, rc = g.in_rows, g.conv_rows
    groups, size = g.groups, g.group_size
    part_blocks = half // groups

    def spot_of(column):
        return sum((column == q).astype(jnp.int32) * g.spot[q] for q in range(L))

    def place(index, order):
        member = lax.rem(index, E)
        spot = spot_of(lax.rem(lax.div(index, E), L))
        row = lax.div(index, E * L)
        row_core, row_y = lax.rem(row, g.cores), lax.div(row, g.cores)
        outer = member * Y + row_y if order == "ens" else row_y * E + member
        return row_core, (lax.div(spot, size) * (E * Y) + outer) * size + lax.rem(spot, size)

    def io_blocks(i, _):
        cols = pl.ds(pl.multiple_of(i * C, 128), C)
        left = mm(pgrad[:, cols], blended[...], (0, 0))
        right = mm(hidden[:, cols], cot_band[...].reshape(g.cells, C), (0, 0))
        for c in range(C // ri):
            where, flat = place(i * (C // ri) + c, "ens")
            both = jnp.concatenate([left[c * ri:(c + 1) * ri], right[c * ri:(c + 1) * ri]], 0)
            io_g[where, flat] = both.astype(BF16)
        return 0

    def conv_blocks(i, _):
        cols = pl.ds(pl.multiple_of(i * C, 128), C)
        product = mm(spread[:, cols], bgrad[...], (0, 0))
        for c in range(C // rc):
            where, flat = place(i * (C // rc) + c, "lat")
            conv_g[where, flat] = product[c * rc:(c + 1) * rc].astype(BF16)
        return 0

    def core_copies(src, dst, index):
        return [
            remote(src.at[1 - core, pl.ds(h * part_blocks, part_blocks)],
                   dst.at[pl.ds(h * part_blocks, part_blocks)],
                   core_send.at[index, h], core_recv.at[index, h],
                   lat=y * g.cores + 1 - core)
            for h in range(groups)
        ]

    def core_sum(total, own, other, h):
        def one(i, _):
            block = own[core, i].astype(F32)
            if g.cores > 1:
                block = block + other[i].astype(F32)
            total[i] = block.astype(BF16)
            return 0
        lax.fori_loop(h * part_blocks, (h + 1) * part_blocks, one, 0)

    def stage(axis):
        if axis == "ens":
            return E, e, [({"ens": lax.rem(e + d, E)}, lax.rem(e + d, E)) for d in range(1, E)]
        turns = [lax.rem(y + d, Y) for d in range(1, Y)]
        return Y, y, [({"lat": p * g.cores + core}, p) for p in turns]

    def stage_start(axis, src, first, dst, h, sem_row):
        n, _, peers = stage(axis)
        m = dst.shape[2]
        copies = []
        for d, (device, p) in enumerate(peers):
            copy = remote(src.at[pl.ds(first + p * m, m)], dst.at[h, d],
                          st_send.at[sem_row, h, d], st_recv.at[sem_row, h, d], **device)
            copy.start()
            copies.append(copy)
        return copies

    def stage_sum(axis, src, first, dst, total, h, copies):
        n, me, _ = stage(axis)
        m = dst.shape[2]
        for copy in copies:
            copy.wait()

        def one(i, _):
            block = src[first + me * m + i].astype(F32)
            for d in range(n - 1):
                block = block + dst[h, d, i].astype(F32)
            total[h * m + i] = block.astype(BF16)
            return 0

        lax.fori_loop(0, m, one, 0)

    def lon_copy(src, dst, d, sem_row):
        p = lax.rem(j + d, L)
        return p, remote(src.at[spot_of(p)], dst.at[d - 1],
                         lon_send.at[sem_row, d - 1], lon_recv.at[sem_row, d - 1], lon=p)

    def lon_start(src, dst, h, sem_row):
        for d in range(1, L):
            p, copy = lon_copy(src, dst, d, sem_row)

            @pl.when(lax.div(spot_of(p), size) == h)
            def _():
                copy.start()

    def lon_sum(src, dst, total, sem_row):
        block = src[spot_of(j)].astype(F32)
        for d in range(1, L):
            lon_copy(src, dst, d, sem_row)[1].wait()
            block = block + dst[d - 1].astype(F32)
        total[...] = block

    lax.fori_loop(0, g.hidden // C, io_blocks, 0)
    io_core = core_copies(io_g, io_c, 0)
    conv_core = core_copies(conv_g, conv_c, 1)
    if g.cores > 1:
        for copy in io_core:
            copy.start()
    bgrad[...] = (
        cot_band[...].reshape(g.cells, C).astype(F32) + mm(pgrad[...], w_in[...], (1, 1))
    ).astype(BF16)
    io_1, conv_1, io_2, conv_2 = ([None] * groups for _ in range(4))
    for h in range(groups):
        if g.cores > 1:
            io_core[h].wait()
        core_sum(io_s0, io_g, io_c, h)
        io_1[h] = stage_start("ens", io_s0, h * part_blocks, io_r1, h, 0)
    lax.fori_loop(0, K, conv_blocks, 0)
    if g.cores > 1:
        for copy in conv_core:
            copy.start()
    bo_band[...] = (
        blended[...].astype(F32) + mm(hidden[...], w_out[...], (1, 0))
    ).astype(BF16).reshape(s, NL, C)
    sends += send_tiles(bo_band, block_out, bo_send, bo_recv)
    for h in range(groups):
        if g.cores > 1:
            conv_core[h].wait()
        core_sum(conv_s0, conv_g, conv_c, h)
        conv_1[h] = stage_start("lat", conv_s0, h * part_blocks, conv_r1, h, 1)

    sgrad[...] = mm(bgrad[...], conv_w[...], (1, 1)).astype(BF16)
    for r in range(s):
        grad = jnp.concatenate(
            [sgrad[r * NL:(r + 1) * NL, k * C:(k + 1) * C] for k in range(K)], 0)
        part = mm(matrix[r], grad, (0, 0)).reshape(g.span, NL, C)
        if r == 0:
            adj[0:g.span] = part
            adj[g.span:] = jnp.zeros((s - 1, NL, C), F32)
        else:
            adj[r:r + g.span] += part

    rim_send[0] = adj[0:rr].astype(BF16)
    rim_send[1] = adj[rr + s:].astype(BF16)
    before = lax.rem(b + last, last + 1)
    after = lax.rem(b + 1, last + 1)
    rims = [
        remote(rim_send.at[0], rim_recv.at[0], rim_ssem.at[0], rim_rsem.at[0],
               lat=lax.div(before, L), lon=lax.rem(before, L)),
        remote(rim_send.at[1], rim_recv.at[1], rim_ssem.at[1], rim_rsem.at[1],
               lat=lax.div(after, L), lon=lax.rem(after, L)),
    ]
    for copy in rims:
        copy.start()

    def return_fields():
        for copy in rims:
            copy.wait()
        from_next = jnp.where(b == last, 0.0, rim_recv[0].astype(F32))
        from_prev = jnp.where(b == 0, 0.0, rim_recv[1].astype(F32))
        adj[rr:2 * rr] += from_prev
        adj[s:s + rr] += from_next
        fg_band[...] = (
            bgrad[...].astype(F32).reshape(s, NL, C) + adj[rr:rr + s]
        ).astype(BF16)
        return send_tiles(fg_band, field_grad, fg_send, fg_recv)

    for h in range(groups):
        stage_sum("ens", io_s0, h * part_blocks, io_r1, io_s1, h, io_1[h])
        io_2[h] = stage_start("lat", io_s1, h * Y * size, io_r2, h, 2)
        if h == 0:
            sends += return_fields()
        stage_sum("lat", conv_s0, h * part_blocks, conv_r1, conv_s1, h, conv_1[h])
        conv_2[h] = stage_start("ens", conv_s1, h * E * size, conv_r2, h, 3)
    for h in range(groups):
        stage_sum("lat", io_s1, h * Y * size, io_r2, io_s2, h, io_2[h])
        lon_start(io_s2, io_r3, h, 0)
        stage_sum("ens", conv_s1, h * E * size, conv_r2, conv_s2, h, conv_2[h])
        lon_start(conv_s2, conv_r3, h, 1)
    await_tiles(block_out, bo_send, bo_recv)
    await_tiles(field_grad, fg_send, fg_recv)
    lon_sum(io_s2, io_r3, io_out, 0)
    lon_sum(conv_s2, conv_r3, conv_out, 1)
    for copy in sends:
        copy.wait_send()


def finish(rows, factor, bo, fg, conv, io, block_out, field_grad, conv_grad, in_grad, out_grad):
    block_out[...] = bo[...]
    field_grad[...] = fg[...]
    conv_grad[...] = conv[...] * factor
    lanes = -(-rows // 128) * 128
    wide = jnp.concatenate([io[:rows], jnp.zeros((lanes - rows, io.shape[1]), F32)], 0)
    in_grad[...] = wide.T[:, :rows] * factor
    out_grad[...] = io[rows:] * factor


def shards(fields, filter_basis, lon_offsets, conv_weight, weight_in, weight_out, cotangent):
    g = Plan(fields, filter_basis, weight_in)
    C, H, K, L, s = g.embed, g.hidden, g.basis, g.lon, g.band
    table = jnp.concatenate(
        [lon_offsets.astype(F32)[:, :, None, :], filter_basis.astype(F32)], axis=2)
    table = table.transpose(0, 2, 3, 1).reshape(s, (K + 1) * g.taps, g.span)
    table = jnp.repeat(table, g.nlon, axis=2)

    vmem, dma = pltpu.VMEM, pltpu.SemaphoreType.DMA
    rc, rio, half = g.conv_rows, 2 * g.in_rows, g.half
    peers = max(g.rows, g.members, 2) - 1

    def slots(n):
        return max(n - 1, 1)

    after_ens, after_lat = half // g.members, half // g.rows
    scratch = [
        vmem(table.shape, F32), vmem((K * C, C), BF16), vmem((C, H), BF16), vmem((H, C), BF16),
        vmem((s + 2 * g.reach, g.nlon, C), BF16), vmem((s, g.nlon, C), BF16),
        vmem((s, K * g.nlon, g.span * g.nlon), BF16), vmem((g.cells, K * C), BF16),
        vmem((g.cells, C), BF16), vmem((g.cells, H), BF16), vmem((g.cells, H), BF16),
        vmem((g.cells, C), BF16), vmem((g.cells, K * C), BF16),
        vmem((s + 2 * g.reach, g.nlon, C), F32),
        vmem((s, g.nlon, C), BF16), vmem((s, g.nlon, C), BF16),
        vmem((2, g.reach, g.nlon, C), BF16), vmem((2, g.reach, g.nlon, C), BF16),
        vmem((g.cores, half, rc, C), BF16), vmem((g.cores, half, rio, C), BF16),
        vmem((half, rc, C), BF16), vmem((half, rio, C), BF16),
        vmem((half, rc, C), BF16), vmem((half, rio, C), BF16),
        vmem((g.groups, slots(g.rows), after_lat // g.groups, rc, C), BF16),
        vmem((g.groups, slots(g.members), after_ens // g.groups, rio, C), BF16),
        vmem((after_lat, rc, C), BF16), vmem((after_ens, rio, C), BF16),
        vmem((g.groups, slots(g.members), g.group_size, rc, C), BF16),
        vmem((g.groups, slots(g.rows), g.group_size, rio, C), BF16),
        vmem((L, rc, C), BF16), vmem((L, rio, C), BF16),
        vmem((slots(L), rc, C), BF16), vmem((slots(L), rio, C), BF16),
        dma((6,)), dma((slots(L), 3)), dma((slots(L), 3)), dma((4,)),
        dma((slots(L),)), dma((slots(L),)), dma((slots(L),)), dma((slots(L),)),
        dma((slots(L),)), dma((slots(L),)), dma((2,)), dma((2,)),
        dma((2, g.groups)), dma((2, g.groups)),
        dma((4, g.groups, peers)), dma((4, g.groups, peers)),
        dma((2, slots(L))), dma((2, slots(L))),
    ]
    in_vmem = pl.BlockSpec(memory_space=pltpu.VMEM)
    anywhere = pl.BlockSpec(memory_space=pl.ANY)
    block_out, field_grad, conv_sum, io_sum = pl.pallas_call(
        functools.partial(kernel, g),
        out_shape=(
            jax.ShapeDtypeStruct(fields.shape, BF16),
            jax.ShapeDtypeStruct(fields.shape, BF16),
            jax.ShapeDtypeStruct((rc, C), F32),
            jax.ShapeDtypeStruct((rio, C), F32),
        ),
        in_specs=[anywhere] * 6,
        out_specs=(in_vmem,) * 4,
        scratch_shapes=scratch,
        compiler_params=pltpu.CompilerParams(
            collective_id=0, has_side_effects=True, vmem_limit_bytes=56 * 1024 * 1024),
        cost_estimate=pl.CostEstimate(
            flops=24 * g.cells * C * H, bytes_accessed=16 * C * H, transcendentals=2 * g.cells * H),
    )(table, fields, cotangent, conv_weight, weight_in, weight_out)

    factor = 1.0 / math.sqrt(g.ens * g.lat * L * g.cells)
    rows = g.in_rows
    if g.members == g.ens:
        return pl.pallas_call(
            functools.partial(finish, rows, factor),
            out_shape=(
                jax.ShapeDtypeStruct(fields.shape, BF16),
                jax.ShapeDtypeStruct(fields.shape, BF16),
                jax.ShapeDtypeStruct((rc, C), F32),
                jax.ShapeDtypeStruct((C, rows), F32),
                jax.ShapeDtypeStruct((rows, C), F32),
            ),
            in_specs=[in_vmem] * 4,
            out_specs=(in_vmem,) * 5,
        )(block_out, field_grad, conv_sum, io_sum)
    conv_sum, in_sum, out_sum = (
        lax.psum_scatter(part.astype(BF16), "ens", scatter_dimension=0, tiled=True).astype(F32)
        for part in (conv_sum, io_sum[:rows], io_sum[rows:])
    )
    return (block_out, field_grad, conv_sum * factor, in_sum.T * factor, out_sum * factor)


def solution(mesh):
    tiles = P("ens", "lat", "lon", None)
    bands = ("lat", "lon")
    blocks = ("lat", "lon", "ens")
    return jax.shard_map(
        shards,
        mesh=mesh,
        in_specs=(tiles, P(bands, None, None, None), P(bands, None, None), P(), P(), P(), tiles),
        out_specs=(tiles, tiles, P(blocks, None), P(None, blocks), P(blocks, None)),
        check_vma=False,
    )
```

```python
import functools
import math

import jax
import jax.numpy as jnp
from jax import lax
from jax.experimental import pallas as pl
from jax.experimental.pallas import tpu as pltpu
from jax.sharding import PartitionSpec as P

HALF_ROOT = 0.7071067811865476
GAUSS_NORM = 0.3989422804014327
MESH = pl.DeviceIdType.MESH
F32 = jnp.float32
BF16 = jnp.bfloat16


def mm(left, right, contract):
    return lax.dot_general(left, right, ((contract[:1], contract[1:]), ((), ())),
                           preferred_element_type=F32)


class Plan:
    def __init__(self, fields, filter_basis, weight_in):
        self.lat, self.lon = lax.axis_size("lat"), lax.axis_size("lon")
        self.ens = lax.axis_size("ens")
        _, self.tile, self.width, self.embed = fields.shape
        self.band, self.span, self.basis, self.taps = filter_basis.shape
        self.hidden = weight_in.shape[1]
        self.reach = self.span // 2
        self.nlon = self.lon * self.width
        self.cells = self.band * self.nlon
        self.cores = 2 if self.lat % 2 == 0 else 1
        self.rows = self.lat // self.cores
        self.members = 1
        for members in (self.ens, 1):
            blocks = self.lat * self.lon * members
            conv_rows = self.basis * self.embed // blocks
            in_rows = self.hidden // blocks
            if conv_rows % 16 == 0 and in_rows % 8 == 0 and self.embed % conv_rows == 0:
                self.members = members
                break
        self.blocks = self.lat * self.lon * self.members
        self.conv_rows = self.basis * self.embed // self.blocks
        self.in_rows = self.hidden // self.blocks
        self.half = self.blocks // self.cores
        width = 256
        self.groups = [(c, min(width, self.embed - c)) for c in range(0, self.embed, width)]


def kernel(
    g, basis_hbm, offsets_hbm, fields, cot, conv_hbm, in_hbm, out_hbm,
    block_out, field_grad, conv_out, io_out,
    basis_ref, offsets_ref, taps_ref, conv_w, w_in, w_out, win, cot_band, matrix, spread, blended, hidden, pgrad, bgrad,
    sgrad, adj, bo_band, fg_band, rim_send, rim_recv,
    conv_g, io_g, conv_c, io_c, conv_s0, io_s0, conv_r1, io_r1, conv_s1, io_s1,
    conv_r2, io_r2, conv_s2, io_s2, conv_r3, io_r3,
    local_sem, gather_send, gather_recv, edge_sem, cot_send, cot_recv,
    bo_send, bo_recv, fg_send, fg_recv, rim_ssem, rim_rsem,
    core_send, core_recv, st_send, st_recv, lon_send, lon_recv,
):
    a, j, e = lax.axis_index("lat"), lax.axis_index("lon"), lax.axis_index("ens")
    L, s, W, T, C = g.lon, g.band, g.width, g.tile, g.embed
    rr = g.reach
    core, y = lax.rem(a, g.cores), lax.div(a, g.cores)
    b = a * L + j
    last = g.lat * L - 1

    def remote(src, dst, ssem, rsem, **device):
        return pltpu.make_async_remote_copy(
            src_ref=src, dst_ref=dst, send_sem=ssem, recv_sem=rsem,
            device_id=device, device_id_type=MESH)

    def columns(index):
        return pl.ds(pl.multiple_of(index * W, W), W)

    weights = [
        pltpu.make_async_copy(src, dst, local_sem.at[i])
        for i, (src, dst) in enumerate(((conv_hbm, conv_w), (in_hbm, w_in), (out_hbm, w_out)))
    ]
    own_field = pltpu.make_async_copy(
        fields.at[0, pl.ds(j * s, s)], win.at[pl.ds(rr, s), columns(j)], local_sem.at[3])
    own_cot = pltpu.make_async_copy(
        cot.at[0, pl.ds(j * s, s)], cot_band.at[:, columns(j)], local_sem.at[4])
    basis_copy = pltpu.make_async_copy(basis_hbm, basis_ref, local_sem.at[5])
    offsets_copy = pltpu.make_async_copy(offsets_hbm, offsets_ref, local_sem.at[6])
    basis_copy.start()
    offsets_copy.start()
    own_field.start()
    own_cot.start()

    barrier = pltpu.get_barrier_semaphore()
    count = 0
    for step in (1, g.lat - 1):
        for q in range(L):
            pl.semaphore_signal(barrier, inc=1, device_id_type=MESH,
                                device_id={"lat": lax.rem(a + step, g.lat), "lon": q})
            count += 1
    for d in range(1, L):
        pl.semaphore_signal(barrier, inc=1, device_id_type=MESH,
                            device_id={"lon": lax.rem(j + d, L)})
        count += 1
    for d in range(1, g.rows):
        pl.semaphore_signal(barrier, inc=1, device_id_type=MESH,
                            device_id={"lat": lax.rem(y + d, g.rows) * g.cores + core})
        count += 1
    for d in range(1, g.members):
        pl.semaphore_signal(barrier, inc=1, device_id_type=MESH,
                            device_id={"ens": lax.rem(e + d, g.members)})
        count += 1
    pl.semaphore_wait(barrier, count)

    def low_src(p):
        return fields.at[0, pl.ds(lax.rem(p * s - rr + T, T), rr)]

    def high_src(p):
        return fields.at[0, pl.ds(lax.rem(p * s + s, T), rr)]

    low_rows, mid_rows, high_rows = pl.ds(0, rr), pl.ds(rr, s), pl.ds(rr + s, rr)

    def up(p):
        return lax.rem(a + (p == 0).astype(jnp.int32), g.lat)

    def down(p):
        return lax.rem(a + g.lat - (p == L - 1).astype(jnp.int32), g.lat)

    sends = []
    for d in range(1, L):
        p = lax.rem(j + d, L)
        triple = (
            (fields.at[0, pl.ds(p * s, s)], mid_rows, a),
            (low_src(p), low_rows, up(p)),
            (high_src(p), high_rows, down(p)),
        )
        for i, (src, rows, row) in enumerate(triple):
            copy = remote(src, win.at[rows, columns(j)], gather_send.at[d - 1, i],
                          gather_recv.at[d - 1, i], lat=row, lon=p)
            copy.start()
            sends.append(copy)
    low_local = pltpu.make_async_copy(low_src(j), win.at[low_rows, columns(j)], edge_sem.at[0])
    low_remote = remote(low_src(j), win.at[low_rows, columns(j)], edge_sem.at[2],
                        edge_sem.at[0], lat=lax.rem(a + 1, g.lat))
    high_local = pltpu.make_async_copy(high_src(j), win.at[high_rows, columns(j)], edge_sem.at[1])
    high_remote = remote(high_src(j), win.at[high_rows, columns(j)], edge_sem.at[3],
                         edge_sem.at[1], lat=lax.rem(a + g.lat - 1, g.lat))

    @pl.when(j == 0)
    def _():
        low_remote.start()

    @pl.when(j != 0)
    def _():
        low_local.start()

    @pl.when(j == L - 1)
    def _():
        high_remote.start()

    @pl.when(j != L - 1)
    def _():
        high_local.start()

    for copy in weights:
        copy.start()

    NL, K, TAPS = g.nlon, g.basis, g.taps
    wide = g.span * NL
    step_rows = 16
    steps = NL // step_rows
    places = lax.broadcasted_iota(jnp.int32, (step_rows, wide), 1)
    lines = lax.broadcasted_iota(jnp.int32, (step_rows, wide), 0)

    def build(i, _):
        r, n0 = lax.div(i, steps), lax.rem(i, steps) * step_rows
        gap = lax.rem(lax.rem(places, NL) - lines - n0 + (NL + NL // 2), NL) - NL // 2
        gap = gap.astype(F32)
        sums = [jnp.zeros((step_rows, wide), F32) for _ in range(K)]
        for t in range(TAPS):
            hit = gap == taps_ref[r, pl.ds(t, 1), :]
            for k in range(K):
                value = taps_ref[r, pl.ds(TAPS * (k + 1) + t, 1), :]
                sums[k] = jnp.where(hit, value, sums[k])
        for k in range(K):
            start = pl.multiple_of(k * NL + n0, step_rows)
            matrix[r, pl.ds(start, step_rows), :] = sums[k].astype(BF16)
        return 0

    ones = (lax.broadcasted_iota(jnp.int32, (g.span, wide), 1) // NL
            == lax.broadcasted_iota(jnp.int32, (g.span, wide), 0)).astype(BF16)
    basis_copy.wait()
    offsets_copy.wait()
    for r in range(s):
        taps_ref[r, 0:TAPS] = mm(offsets_ref[:, r, :].astype(F32).astype(BF16), ones, (0, 0))
        for k in range(K):
            taps_ref[r, TAPS * (k + 1):TAPS * (k + 2)] = mm(basis_ref[r, :, k, :], ones, (0, 0))
    lax.fori_loop(0, s * steps, build, 0)
    for d in range(1, L):
        p = lax.rem(j + d, L)
        copy = remote(cot.at[0, pl.ds(p * s, s)], cot_band.at[:, columns(j)],
                      cot_send.at[d - 1], cot_recv.at[d - 1], lon=p)
        copy.start()
        sends.append(copy)

    own_field.wait()
    for d in range(1, L):
        source = lax.rem(j - d + L, L)
        for i, rows in enumerate((mid_rows, low_rows, high_rows)):
            landed = win.at[rows, columns(source)]
            remote(landed, landed, gather_send.at[d - 1, i], gather_recv.at[d - 1, i],
                   lon=source).wait_recv()

    @pl.when(j == 0)
    def _():
        low_remote.wait()

    @pl.when(j != 0)
    def _():
        low_local.wait()

    @pl.when(j == L - 1)
    def _():
        high_remote.wait()

    @pl.when(j != L - 1)
    def _():
        high_local.wait()

    @pl.when(b == 0)
    def _():
        win[0:rr] = jnp.zeros((rr, NL, C), BF16)

    @pl.when(b == last)
    def _():
        win[rr + s:] = jnp.zeros((rr, NL, C), BF16)

    for r in range(s):
        window = win[r:r + g.span].reshape(wide, C)
        part = mm(matrix[r], window, (1, 0)).astype(BF16)
        for k in range(K):
            spread[r * NL:(r + 1) * NL, k * C:(k + 1) * C] = part[k * NL:(k + 1) * NL]
    weights[0].wait()
    blended[...] = (
        win[rr:rr + s].reshape(g.cells, C).astype(F32) + mm(spread[...], conv_w[...], (1, 0))
    ).astype(BF16)

    own_cot.wait()
    for d in range(1, L):
        source = lax.rem(j - d + L, L)
        landed = cot_band.at[:, columns(source)]
        remote(landed, landed, cot_send.at[d - 1], cot_recv.at[d - 1], lon=source).wait_recv()
    weights[1].wait()
    weights[2].wait()
    lanes = 256 if g.hidden % 256 == 0 else g.hidden

    def units(i, _):
        cols = pl.ds(pl.multiple_of(i * lanes, lanes), lanes)
        pre = mm(blended[...], w_in[:, cols], (1, 0))
        cdf = 0.5 * (1.0 + lax.erf(pre * HALF_ROOT))
        hidden[:, cols] = (pre * cdf).astype(BF16)
        hgrad = mm(cot_band[...].reshape(g.cells, C), w_out[cols, :], (1, 1))
        slope = cdf + pre * jnp.exp(-0.5 * pre * pre) * GAUSS_NORM
        pgrad[:, cols] = (hgrad * slope).astype(BF16)
        return 0

    lax.fori_loop(0, g.hidden // lanes, units, 0)

    def send_tiles(band, out, ssem, rsem):
        copies = []
        for d in range(1, L):
            p = lax.rem(j + d, L)
            copy = remote(band.at[:, columns(p)], out.at[0, pl.ds(j * s, s)],
                          ssem.at[d - 1], rsem.at[d - 1], lon=p)
            copy.start()
            copies.append(copy)
        out[0, pl.ds(j * s, s)] = band[:, columns(j), :]
        return copies

    def await_tiles(out, ssem, rsem):
        for d in range(1, L):
            source = lax.rem(j - d + L, L)
            landed = out.at[0, pl.ds(source * s, s)]
            remote(landed, landed, ssem.at[d - 1], rsem.at[d - 1], lon=source).wait_recv()

    E, Y, half = g.members, g.rows, g.half
    ri, rc = g.in_rows, g.conv_rows
    groups = range(len(g.groups))

    def place(index, order):
        member = lax.rem(index, E)
        column = lax.rem(lax.div(index, E), L)
        row = lax.div(index, E * L)
        row_core, row_y = lax.rem(row, g.cores), lax.div(row, g.cores)
        outer = member * Y + row_y if order == "ens" else row_y * E + member
        return row_core, outer * L + column

    def cut(h):
        return pl.ds(*g.groups[h])

    def add(blocks):
        if len(blocks) == 2:
            return blocks[0] + blocks[1]
        return sum((block.astype(F32) for block in blocks[1:]), blocks[0].astype(F32)).astype(BF16)

    def io_blocks(i, _):
        cols = pl.ds(pl.multiple_of(i * C, 128), C)
        left = mm(pgrad[:, cols], blended[...], (0, 0))
        right = mm(hidden[:, cols], cot_band[...].reshape(g.cells, C), (0, 0))
        for c in range(C // ri):
            where, flat = place(i * (C // ri) + c, "ens")
            both = jnp.concatenate([left[c * ri:(c + 1) * ri], right[c * ri:(c + 1) * ri]], 0)
            io_g[where, flat] = both.astype(BF16)
        return 0

    def conv_blocks(i, _):
        cols = pl.ds(pl.multiple_of(i * C, 128), C)
        product = mm(spread[:, cols], bgrad[...], (0, 0))
        for c in range(C // rc):
            where, flat = place(i * (C // rc) + c, "lat")
            conv_g[where, flat] = product[c * rc:(c + 1) * rc].astype(BF16)
        return 0

    def core_copies(src, dst, index):
        return [
            remote(src.at[1 - core, :, :, cut(h)], dst.at[:, :, cut(h)],
                   core_send.at[index, h], core_recv.at[index, h],
                   lat=y * g.cores + 1 - core)
            for h in groups
        ]

    def core_sum(total, own, other, h):
        def one(i, _):
            blocks = [own[core, i, :, cut(h)]]
            if g.cores > 1:
                blocks.append(other[i, :, cut(h)])
            total[i, :, cut(h)] = add(blocks)
            return 0
        lax.fori_loop(0, half, one, 0)

    def stage(axis):
        if axis == "ens":
            return E, e, [({"ens": lax.rem(e + d, E)}, lax.rem(e + d, E)) for d in range(1, E)]
        turns = [lax.rem(y + d, Y) for d in range(1, Y)]
        return Y, y, [({"lat": p * g.cores + core}, p) for p in turns]

    def stage_start(axis, src, dst, h, sem_row):
        _, _, peers = stage(axis)
        m = dst.shape[1]
        copies = []
        for d, (device, p) in enumerate(peers):
            copy = remote(src.at[pl.ds(p * m, m), :, cut(h)], dst.at[d, :, :, cut(h)],
                          st_send.at[sem_row, h, d], st_recv.at[sem_row, h, d], **device)
            copy.start()
            copies.append(copy)
        return copies

    def stage_sum(axis, src, dst, total, h, copies):
        n, me, _ = stage(axis)
        m = dst.shape[1]
        for copy in copies:
            copy.wait()

        def one(i, _):
            total[i, :, cut(h)] = add(
                [src[me * m + i, :, cut(h)]] + [dst[d, i, :, cut(h)] for d in range(n - 1)])
            return 0

        lax.fori_loop(0, m, one, 0)

    def lon_start(src, dst, h, sem_row):
        copies = []
        for d in range(1, L):
            p = lax.rem(j + d, L)
            copy = remote(src.at[p, :, cut(h)], dst.at[d - 1, :, cut(h)],
                          lon_send.at[sem_row, h, d - 1], lon_recv.at[sem_row, h, d - 1], lon=p)
            copy.start()
            copies.append(copy)
        return copies

    def lon_sum(src, dst, total, h, copies):
        block = src[j, :, cut(h)].astype(F32)
        for d, copy in enumerate(copies):
            copy.wait()
            block = block + dst[d, :, cut(h)].astype(F32)
        total[:, cut(h)] = block

    lax.fori_loop(0, g.hidden // C, io_blocks, 0)
    io_core = core_copies(io_g, io_c, 0)
    conv_core = core_copies(conv_g, conv_c, 1)
    if g.cores > 1:
        for copy in io_core:
            copy.start()
    bgrad[...] = (
        cot_band[...].reshape(g.cells, C).astype(F32) + mm(pgrad[...], w_in[...], (1, 1))
    ).astype(BF16)
    io_1, conv_1, io_2, conv_2, io_3, conv_3 = ([None for _ in groups] for _ in range(6))
    for h in groups:
        if g.cores > 1:
            io_core[h].wait()
        core_sum(io_s0, io_g, io_c, h)
        io_1[h] = stage_start("ens", io_s0, io_r1, h, 0)
    lax.fori_loop(0, K, conv_blocks, 0)
    if g.cores > 1:
        for copy in conv_core:
            copy.start()
    bo_band[...] = (
        blended[...].astype(F32) + mm(hidden[...], w_out[...], (1, 0))
    ).astype(BF16).reshape(s, NL, C)
    sends += send_tiles(bo_band, block_out, bo_send, bo_recv)
    for h in groups:
        if g.cores > 1:
            conv_core[h].wait()
        core_sum(conv_s0, conv_g, conv_c, h)
        conv_1[h] = stage_start("lat", conv_s0, conv_r1, h, 1)

    sgrad[...] = mm(bgrad[...], conv_w[...], (1, 1)).astype(BF16)
    for r in range(s):
        grad = jnp.concatenate(
            [sgrad[r * NL:(r + 1) * NL, k * C:(k + 1) * C] for k in range(K)], 0)
        part = mm(matrix[r], grad, (0, 0)).reshape(g.span, NL, C)
        if r == 0:
            adj[0:g.span] = part
            adj[g.span:] = jnp.zeros((s - 1, NL, C), F32)
        else:
            adj[r:r + g.span] += part

    rim_send[0] = adj[0:rr].astype(BF16)
    rim_send[1] = adj[rr + s:].astype(BF16)
    before = lax.rem(b + last, last + 1)
    after = lax.rem(b + 1, last + 1)
    rims = [
        remote(rim_send.at[0], rim_recv.at[0], rim_ssem.at[0], rim_rsem.at[0],
               lat=lax.div(before, L), lon=lax.rem(before, L)),
        remote(rim_send.at[1], rim_recv.at[1], rim_ssem.at[1], rim_rsem.at[1],
               lat=lax.div(after, L), lon=lax.rem(after, L)),
    ]
    for copy in rims:
        copy.start()

    def return_fields():
        for copy in rims:
            copy.wait()
        from_next = jnp.where(b == last, 0.0, rim_recv[0].astype(F32))
        from_prev = jnp.where(b == 0, 0.0, rim_recv[1].astype(F32))
        adj[rr:2 * rr] += from_prev
        adj[s:s + rr] += from_next
        fg_band[...] = (
            bgrad[...].astype(F32).reshape(s, NL, C) + adj[rr:rr + s]
        ).astype(BF16)
        return send_tiles(fg_band, field_grad, fg_send, fg_recv)

    for h in groups:
        stage_sum("ens", io_s0, io_r1, io_s1, h, io_1[h])
        io_2[h] = stage_start("lat", io_s1, io_r2, h, 2)
        if h == min(1, groups[-1]):
            sends += return_fields()
        stage_sum("lat", conv_s0, conv_r1, conv_s1, h, conv_1[h])
        conv_2[h] = stage_start("ens", conv_s1, conv_r2, h, 3)
    for h in groups:
        stage_sum("lat", io_s1, io_r2, io_s2, h, io_2[h])
        io_3[h] = lon_start(io_s2, io_r3, h, 0)
        stage_sum("ens", conv_s1, conv_r2, conv_s2, h, conv_2[h])
        conv_3[h] = lon_start(conv_s2, conv_r3, h, 1)
    await_tiles(block_out, bo_send, bo_recv)
    await_tiles(field_grad, fg_send, fg_recv)
    for h in groups:
        lon_sum(io_s2, io_r3, io_out, h, io_3[h])
        lon_sum(conv_s2, conv_r3, conv_out, h, conv_3[h])
    for copy in sends:
        copy.wait_send()


def finish(rows, factor, bo, fg, conv, io, block_out, field_grad, conv_grad, in_grad, out_grad):
    block_out[...] = bo[...]
    field_grad[...] = fg[...]
    conv_grad[...] = conv[...] * factor
    in_grad[...] = io[:rows] * factor
    out_grad[...] = io[rows:] * factor


def shards(fields, filter_basis, lon_offsets, conv_weight, weight_in, weight_out, cotangent):
    g = Plan(fields, filter_basis, weight_in)
    C, H, K, L, s = g.embed, g.hidden, g.basis, g.lon, g.band
    vmem, dma = pltpu.VMEM, pltpu.SemaphoreType.DMA
    rc, rio, half = g.conv_rows, 2 * g.in_rows, g.half
    peers = max(g.rows, g.members, 2) - 1

    def slots(n):
        return max(n - 1, 1)

    cuts = len(g.groups)
    after_ens, after_lat = half // g.members, half // g.rows
    scratch = [
        vmem(filter_basis.shape, BF16), vmem((g.span, s, g.taps), jnp.int32),
        vmem((s, (K + 1) * g.taps, g.span * g.nlon), F32), vmem((K * C, C), BF16), vmem((C, H), BF16), vmem((H, C), BF16),
        vmem((s + 2 * g.reach, g.nlon, C), BF16), vmem((s, g.nlon, C), BF16),
        vmem((s, K * g.nlon, g.span * g.nlon), BF16), vmem((g.cells, K * C), BF16),
        vmem((g.cells, C), BF16), vmem((g.cells, H), BF16), vmem((g.cells, H), BF16),
        vmem((g.cells, C), BF16), vmem((g.cells, K * C), BF16),
        vmem((s + 2 * g.reach, g.nlon, C), F32),
        vmem((s, g.nlon, C), BF16), vmem((s, g.nlon, C), BF16),
        vmem((2, g.reach, g.nlon, C), BF16), vmem((2, g.reach, g.nlon, C), BF16),
        vmem((g.cores, half, rc, C), BF16), vmem((g.cores, half, rio, C), BF16),
        vmem((half, rc, C), BF16), vmem((half, rio, C), BF16),
        vmem((half, rc, C), BF16), vmem((half, rio, C), BF16),
        vmem((slots(g.rows), after_lat, rc, C), BF16),
        vmem((slots(g.members), after_ens, rio, C), BF16),
        vmem((after_lat, rc, C), BF16), vmem((after_ens, rio, C), BF16),
        vmem((slots(g.members), L, rc, C), BF16), vmem((slots(g.rows), L, rio, C), BF16),
        vmem((L, rc, C), BF16), vmem((L, rio, C), BF16),
        vmem((slots(L), rc, C), BF16), vmem((slots(L), rio, C), BF16),
        dma((7,)), dma((slots(L), 3)), dma((slots(L), 3)), dma((4,)),
        dma((slots(L),)), dma((slots(L),)), dma((slots(L),)), dma((slots(L),)),
        dma((slots(L),)), dma((slots(L),)), dma((2,)), dma((2,)),
        dma((2, cuts)), dma((2, cuts)), dma((4, cuts, peers)), dma((4, cuts, peers)),
        dma((2, cuts, slots(L))), dma((2, cuts, slots(L))),
    ]
    in_vmem = pl.BlockSpec(memory_space=pltpu.VMEM)
    anywhere = pl.BlockSpec(memory_space=pl.ANY)
    block_out, field_grad, conv_sum, io_sum = pl.pallas_call(
        functools.partial(kernel, g),
        out_shape=(
            jax.ShapeDtypeStruct(fields.shape, BF16),
            jax.ShapeDtypeStruct(fields.shape, BF16),
            jax.ShapeDtypeStruct((rc, C), F32),
            jax.ShapeDtypeStruct((rio, C), F32),
        ),
        in_specs=[anywhere] * 7,
        out_specs=(in_vmem,) * 4,
        scratch_shapes=scratch,
        compiler_params=pltpu.CompilerParams(
            collective_id=0, has_side_effects=True, vmem_limit_bytes=56 * 1024 * 1024),
        cost_estimate=pl.CostEstimate(
            flops=24 * g.cells * C * H, bytes_accessed=16 * C * H, transcendentals=2 * g.cells * H),
    )(filter_basis, lon_offsets.transpose(1, 0, 2), fields, cotangent, conv_weight, weight_in, weight_out)

    factor = 1.0 / math.sqrt(g.ens * g.lat * L * g.cells)
    rows = g.in_rows
    if g.members == g.ens:
        outs = pl.pallas_call(
            functools.partial(finish, rows, factor),
            out_shape=(
                jax.ShapeDtypeStruct(fields.shape, BF16),
                jax.ShapeDtypeStruct(fields.shape, BF16),
                jax.ShapeDtypeStruct((rc, C), F32),
                jax.ShapeDtypeStruct((rows, C), F32),
                jax.ShapeDtypeStruct((rows, C), F32),
            ),
            in_specs=[in_vmem] * 4,
            out_specs=(in_vmem,) * 5,
        )(block_out, field_grad, conv_sum, io_sum)
        return outs[:3] + (outs[3].T, outs[4])
    conv_sum, in_sum, out_sum = (
        lax.psum_scatter(part.astype(BF16), "ens", scatter_dimension=0, tiled=True).astype(F32)
        for part in (conv_sum, io_sum[:rows], io_sum[rows:])
    )
    return (block_out, field_grad, conv_sum * factor, in_sum.T * factor, out_sum * factor)


def solution(mesh):
    tiles = P("ens", "lat", "lon", None)
    bands = ("lat", "lon")
    blocks = ("lat", "lon", "ens")
    return jax.shard_map(
        shards,
        mesh=mesh,
        in_specs=(tiles, P(bands, None, None, None), P(bands, None, None), P(), P(), P(), tiles),
        out_specs=(tiles, tiles, P(blocks, None), P(None, blocks), P(blocks, None)),
        check_vma=False,
    )
```

```python
import functools
import math

import jax
import jax.numpy as jnp
from jax import lax
from jax.experimental import pallas as pl
from jax.experimental.pallas import tpu as pltpu
from jax.sharding import PartitionSpec as P

HALF_ROOT = 0.7071067811865476
GAUSS_NORM = 0.3989422804014327
MESH = pl.DeviceIdType.MESH
F32 = jnp.float32
BF16 = jnp.bfloat16


def mm(left, right, contract):
    return lax.dot_general(left, right, ((contract[:1], contract[1:]), ((), ())),
                           preferred_element_type=F32)


class Plan:
    def __init__(self, fields, filter_basis, weight_in):
        self.lat, self.lon = lax.axis_size("lat"), lax.axis_size("lon")
        self.ens = lax.axis_size("ens")
        _, self.tile, self.width, self.embed = fields.shape
        self.band, self.span, self.basis, self.taps = filter_basis.shape
        self.hidden = weight_in.shape[1]
        self.reach = self.span // 2
        self.nlon = self.lon * self.width
        self.cells = self.band * self.nlon
        self.cores = 2 if self.lat % 2 == 0 else 1
        self.rows = self.lat // self.cores
        self.members = 1
        for members in (self.ens, 1):
            blocks = self.lat * self.lon * members
            conv_rows = self.basis * self.embed // blocks
            in_rows = self.hidden // blocks
            if conv_rows % 16 == 0 and in_rows % 8 == 0 and self.embed % conv_rows == 0:
                self.members = members
                break
        self.blocks = self.lat * self.lon * self.members
        self.conv_rows = self.basis * self.embed // self.blocks
        self.in_rows = self.hidden // self.blocks
        self.half = self.blocks // self.cores
        width = 256
        self.groups = [(c, min(width, self.embed - c)) for c in range(0, self.embed, width)]


def kernel(
    g, basis_hbm, offsets_hbm, fields, cot, conv_hbm, in_hbm, out_hbm,
    block_out, field_grad, conv_out, io_out,
    basis_ref, offsets_ref, taps_ref, conv_w, w_in, w_out, win, cot_band, matrix, spread, blended, hidden, pgrad, bgrad,
    sgrad, adj, bo_band, fg_band, rim_send, rim_recv,
    conv_g, io_g, conv_c, io_c, conv_s0, io_s0, conv_r1, io_r1, conv_s1, io_s1,
    conv_r2, io_r2, conv_s2, io_s2, conv_r3, io_r3,
    local_sem, gather_send, gather_recv, edge_sem, cot_send, cot_recv,
    bo_send, bo_recv, fg_send, fg_recv, rim_ssem, rim_rsem,
    core_send, core_recv, st_send, st_recv, lon_send, lon_recv,
):
    a, j, e = lax.axis_index("lat"), lax.axis_index("lon"), lax.axis_index("ens")
    L, s, W, T, C = g.lon, g.band, g.width, g.tile, g.embed
    rr = g.reach
    core, y = lax.rem(a, g.cores), lax.div(a, g.cores)
    b = a * L + j
    last = g.lat * L - 1

    def remote(src, dst, ssem, rsem, **device):
        return pltpu.make_async_remote_copy(
            src_ref=src, dst_ref=dst, send_sem=ssem, recv_sem=rsem,
            device_id=device, device_id_type=MESH)

    def columns(index):
        return pl.ds(pl.multiple_of(index * W, W), W)

    weights = [
        pltpu.make_async_copy(src, dst, local_sem.at[i])
        for i, (src, dst) in enumerate(((conv_hbm, conv_w), (in_hbm, w_in), (out_hbm, w_out)))
    ]
    own_field = pltpu.make_async_copy(
        fields.at[0, pl.ds(j * s, s)], win.at[pl.ds(rr, s), columns(j)], local_sem.at[3])
    own_cot = pltpu.make_async_copy(
        cot.at[0, pl.ds(j * s, s)], cot_band.at[:, columns(j)], local_sem.at[4])
    basis_copy = pltpu.make_async_copy(basis_hbm, basis_ref, local_sem.at[5])
    offsets_copy = pltpu.make_async_copy(offsets_hbm, offsets_ref, local_sem.at[6])
    basis_copy.start()
    offsets_copy.start()
    own_field.start()
    own_cot.start()

    barrier = pltpu.get_barrier_semaphore()
    count = 0
    for step in (1, g.lat - 1):
        for q in range(L):
            pl.semaphore_signal(barrier, inc=1, device_id_type=MESH,
                                device_id={"lat": lax.rem(a + step, g.lat), "lon": q})
            count += 1
    for d in range(1, L):
        pl.semaphore_signal(barrier, inc=1, device_id_type=MESH,
                            device_id={"lon": lax.rem(j + d, L)})
        count += 1
    for d in range(1, g.rows):
        pl.semaphore_signal(barrier, inc=1, device_id_type=MESH,
                            device_id={"lat": lax.rem(y + d, g.rows) * g.cores + core})
        count += 1
    for d in range(1, g.members):
        pl.semaphore_signal(barrier, inc=1, device_id_type=MESH,
                            device_id={"ens": lax.rem(e + d, g.members)})
        count += 1
    pl.semaphore_wait(barrier, count)

    def low_src(p):
        return fields.at[0, pl.ds(lax.rem(p * s - rr + T, T), rr)]

    def high_src(p):
        return fields.at[0, pl.ds(lax.rem(p * s + s, T), rr)]

    low_rows, mid_rows, high_rows = pl.ds(0, rr), pl.ds(rr, s), pl.ds(rr + s, rr)

    def up(p):
        return lax.rem(a + (p == 0).astype(jnp.int32), g.lat)

    def down(p):
        return lax.rem(a + g.lat - (p == L - 1).astype(jnp.int32), g.lat)

    sends = []
    for d in range(1, L):
        p = lax.rem(j + d, L)
        triple = (
            (fields.at[0, pl.ds(p * s, s)], mid_rows, a),
            (low_src(p), low_rows, up(p)),
            (high_src(p), high_rows, down(p)),
        )
        for i, (src, rows, row) in enumerate(triple):
            copy = remote(src, win.at[rows, columns(j)], gather_send.at[d - 1, i],
                          gather_recv.at[d - 1, i], lat=row, lon=p)
            copy.start()
            sends.append(copy)
    low_local = pltpu.make_async_copy(low_src(j), win.at[low_rows, columns(j)], edge_sem.at[0])
    low_remote = remote(low_src(j), win.at[low_rows, columns(j)], edge_sem.at[2],
                        edge_sem.at[0], lat=lax.rem(a + 1, g.lat))
    high_local = pltpu.make_async_copy(high_src(j), win.at[high_rows, columns(j)], edge_sem.at[1])
    high_remote = remote(high_src(j), win.at[high_rows, columns(j)], edge_sem.at[3],
                         edge_sem.at[1], lat=lax.rem(a + g.lat - 1, g.lat))

    @pl.when(j == 0)
    def _():
        low_remote.start()

    @pl.when(j != 0)
    def _():
        low_local.start()

    @pl.when(j == L - 1)
    def _():
        high_remote.start()

    @pl.when(j != L - 1)
    def _():
        high_local.start()

    for copy in weights:
        copy.start()

    NL, K, TAPS = g.nlon, g.basis, g.taps
    wide = g.span * NL
    step_rows = 16
    steps = NL // step_rows
    places = lax.broadcasted_iota(jnp.int32, (step_rows, wide), 1)
    lines = lax.broadcasted_iota(jnp.int32, (step_rows, wide), 0)

    def build(i, _):
        r, n0 = lax.div(i, steps), lax.rem(i, steps) * step_rows
        gap = lax.rem(lax.rem(places, NL) - lines - n0 + (NL + NL // 2), NL) - NL // 2
        gap = gap.astype(F32)
        sums = [jnp.zeros((step_rows, wide), F32) for _ in range(K)]
        for t in range(TAPS):
            hit = gap == taps_ref[r, pl.ds(t, 1), :]
            for k in range(K):
                value = taps_ref[r, pl.ds(TAPS * (k + 1) + t, 1), :]
                sums[k] = jnp.where(hit, value, sums[k])
        for k in range(K):
            start = pl.multiple_of(k * NL + n0, step_rows)
            matrix[r, pl.ds(start, step_rows), :] = sums[k].astype(BF16)
        return 0

    ones = (lax.broadcasted_iota(jnp.int32, (g.span, wide), 1) // NL
            == lax.broadcasted_iota(jnp.int32, (g.span, wide), 0)).astype(BF16)
    basis_copy.wait()
    offsets_copy.wait()
    for r in range(s):
        taps_ref[r, 0:TAPS] = mm(offsets_ref[:, r, :].astype(F32).astype(BF16), ones, (0, 0))
        for k in range(K):
            taps_ref[r, TAPS * (k + 1):TAPS * (k + 2)] = mm(basis_ref[r, :, k, :], ones, (0, 0))
    lax.fori_loop(0, s * steps, build, 0)

    own_field.wait()
    for d in range(1, L):
        source = lax.rem(j - d + L, L)
        for i, rows in enumerate((mid_rows, low_rows, high_rows)):
            landed = win.at[rows, columns(source)]
            remote(landed, landed, gather_send.at[d - 1, i], gather_recv.at[d - 1, i],
                   lon=source).wait_recv()

    @pl.when(j == 0)
    def _():
        low_remote.wait()

    @pl.when(j != 0)
    def _():
        low_local.wait()

    @pl.when(j == L - 1)
    def _():
        high_remote.wait()

    @pl.when(j != L - 1)
    def _():
        high_local.wait()

    for d in range(1, L):
        p = lax.rem(j + d, L)
        copy = remote(cot.at[0, pl.ds(p * s, s)], cot_band.at[:, columns(j)],
                      cot_send.at[d - 1], cot_recv.at[d - 1], lon=p)
        copy.start()
        sends.append(copy)

    @pl.when(b == 0)
    def _():
        win[0:rr] = jnp.zeros((rr, NL, C), BF16)

    @pl.when(b == last)
    def _():
        win[rr + s:] = jnp.zeros((rr, NL, C), BF16)

    for r in range(s):
        window = win[r:r + g.span].reshape(wide, C)
        part = mm(matrix[r], window, (1, 0)).astype(BF16)
        for k in range(K):
            spread[r * NL:(r + 1) * NL, k * C:(k + 1) * C] = part[k * NL:(k + 1) * NL]
    weights[0].wait()
    blended[...] = (
        win[rr:rr + s].reshape(g.cells, C).astype(F32) + mm(spread[...], conv_w[...], (1, 0))
    ).astype(BF16)

    own_cot.wait()
    for d in range(1, L):
        source = lax.rem(j - d + L, L)
        landed = cot_band.at[:, columns(source)]
        remote(landed, landed, cot_send.at[d - 1], cot_recv.at[d - 1], lon=source).wait_recv()
    weights[1].wait()
    weights[2].wait()
    lanes = 256 if g.hidden % 256 == 0 else g.hidden

    def units(i, _):
        cols = pl.ds(pl.multiple_of(i * lanes, lanes), lanes)
        pre = mm(blended[...], w_in[:, cols], (1, 0))
        cdf = 0.5 * (1.0 + lax.erf(pre * HALF_ROOT))
        hidden[:, cols] = (pre * cdf).astype(BF16)
        hgrad = mm(cot_band[...].reshape(g.cells, C), w_out[cols, :], (1, 1))
        slope = cdf + pre * jnp.exp(-0.5 * pre * pre) * GAUSS_NORM
        pgrad[:, cols] = (hgrad * slope).astype(BF16)
        return 0

    lax.fori_loop(0, g.hidden // lanes, units, 0)

    def send_tiles(band, out, ssem, rsem):
        copies = []
        for d in range(1, L):
            p = lax.rem(j + d, L)
            copy = remote(band.at[:, columns(p)], out.at[0, pl.ds(j * s, s)],
                          ssem.at[d - 1], rsem.at[d - 1], lon=p)
            copy.start()
            copies.append(copy)
        out[0, pl.ds(j * s, s)] = band[:, columns(j), :]
        return copies

    def await_tiles(out, ssem, rsem):
        for d in range(1, L):
            source = lax.rem(j - d + L, L)
            landed = out.at[0, pl.ds(source * s, s)]
            remote(landed, landed, ssem.at[d - 1], rsem.at[d - 1], lon=source).wait_recv()

    E, Y, half = g.members, g.rows, g.half
    ri, rc = g.in_rows, g.conv_rows
    groups = range(len(g.groups))

    def place(index, order):
        member = lax.rem(index, E)
        column = lax.rem(lax.div(index, E), L)
        row = lax.div(index, E * L)
        row_core, row_y = lax.rem(row, g.cores), lax.div(row, g.cores)
        outer = member * Y + row_y if order == "ens" else row_y * E + member
        return row_core, outer * L + column

    def cut(h):
        return pl.ds(*g.groups[h])

    def add(blocks):
        if len(blocks) == 2:
            return blocks[0] + blocks[1]
        return sum((block.astype(F32) for block in blocks[1:]), blocks[0].astype(F32)).astype(BF16)

    def io_blocks(i, _):
        cols = pl.ds(pl.multiple_of(i * C, 128), C)
        left = mm(pgrad[:, cols], blended[...], (0, 0))
        right = mm(hidden[:, cols], cot_band[...].reshape(g.cells, C), (0, 0))
        for c in range(C // ri):
            where, flat = place(i * (C // ri) + c, "ens")
            both = jnp.concatenate([left[c * ri:(c + 1) * ri], right[c * ri:(c + 1) * ri]], 0)
            io_g[where, flat] = both.astype(BF16)
        return 0

    def conv_blocks(i, _):
        cols = pl.ds(pl.multiple_of(i * C, 128), C)
        product = mm(spread[:, cols], bgrad[...], (0, 0))
        for c in range(C // rc):
            where, flat = place(i * (C // rc) + c, "lat")
            conv_g[where, flat] = product[c * rc:(c + 1) * rc].astype(BF16)
        return 0

    def core_copies(src, dst, index):
        return [
            remote(src.at[1 - core, :, :, cut(h)], dst.at[:, :, cut(h)],
                   core_send.at[index, h], core_recv.at[index, h],
                   lat=y * g.cores + 1 - core)
            for h in groups
        ]

    def core_sum(total, own, other, h):
        def one(i, _):
            blocks = [own[core, i, :, cut(h)]]
            if g.cores > 1:
                blocks.append(other[i, :, cut(h)])
            total[i, :, cut(h)] = add(blocks)
            return 0
        lax.fori_loop(0, half, one, 0)

    def stage(axis):
        if axis == "ens":
            return E, e, [({"ens": lax.rem(e + d, E)}, lax.rem(e + d, E)) for d in range(1, E)]
        turns = [lax.rem(y + d, Y) for d in range(1, Y)]
        return Y, y, [({"lat": p * g.cores + core}, p) for p in turns]

    def stage_start(axis, src, dst, h, sem_row):
        _, _, peers = stage(axis)
        m = dst.shape[1]
        copies = []
        for d, (device, p) in enumerate(peers):
            copy = remote(src.at[pl.ds(p * m, m), :, cut(h)], dst.at[d, :, :, cut(h)],
                          st_send.at[sem_row, h, d], st_recv.at[sem_row, h, d], **device)
            copy.start()
            copies.append(copy)
        return copies

    def stage_sum(axis, src, dst, total, h):
        n, me, _ = stage(axis)
        m = dst.shape[1]

        def one(i, _):
            total[i, :, cut(h)] = add(
                [src[me * m + i, :, cut(h)]] + [dst[d, i, :, cut(h)] for d in range(n - 1)])
            return 0

        lax.fori_loop(0, m, one, 0)

    def lon_start(src, dst, h, sem_row):
        copies = []
        for d in range(1, L):
            p = lax.rem(j + d, L)
            copy = remote(src.at[p, :, cut(h)], dst.at[d - 1, :, cut(h)],
                          lon_send.at[sem_row, h, d - 1], lon_recv.at[sem_row, h, d - 1], lon=p)
            copy.start()
            copies.append(copy)
        return copies

    def lon_sum(src, dst, total, h, copies):
        block = src[j, :, cut(h)].astype(F32)
        for d, copy in enumerate(copies):
            copy.wait()
            block = block + dst[d, :, cut(h)].astype(F32)
        total[:, cut(h)] = block

    lax.fori_loop(0, g.hidden // C, io_blocks, 0)
    io_core = core_copies(io_g, io_c, 0)
    conv_core = core_copies(conv_g, conv_c, 1)
    if g.cores > 1:
        io_core[0].start()
    bgrad[...] = (
        cot_band[...].reshape(g.cells, C).astype(F32) + mm(pgrad[...], w_in[...], (1, 1))
    ).astype(BF16)
    io_1, conv_1, io_2, conv_2, io_3, conv_3 = ([None for _ in groups] for _ in range(6))

    def after_core(copies, total, own, other, h):
        if g.cores > 1:
            copies[h].wait()
        core_sum(total, own, other, h)

    def start_rest(copies):
        if g.cores > 1:
            for copy in copies[1:]:
                copy.start()

    def finish_stage(copies):
        for copy in copies:
            copy.wait()

    start_rest(io_core)
    after_core(io_core, io_s0, io_g, io_c, 0)
    io_1[0] = stage_start("ens", io_s0, io_r1, 0, 0)
    lax.fori_loop(0, K, conv_blocks, 0)
    if g.cores > 1:
        conv_core[0].start()
    bo_band[...] = (
        blended[...].astype(F32) + mm(hidden[...], w_out[...], (1, 0))
    ).astype(BF16).reshape(s, NL, C)
    sends += send_tiles(bo_band, block_out, bo_send, bo_recv)
    start_rest(conv_core)
    after_core(conv_core, conv_s0, conv_g, conv_c, 0)
    conv_1[0] = stage_start("lat", conv_s0, conv_r1, 0, 1)

    sgrad[...] = mm(bgrad[...], conv_w[...], (1, 1)).astype(BF16)
    for r in range(s):
        grad = jnp.concatenate(
            [sgrad[r * NL:(r + 1) * NL, k * C:(k + 1) * C] for k in range(K)], 0)
        part = mm(matrix[r], grad, (0, 0)).reshape(g.span, NL, C)
        if r == 0:
            adj[0:g.span] = part
            adj[g.span:] = jnp.zeros((s - 1, NL, C), F32)
        else:
            adj[r:r + g.span] += part

    rim_send[0] = adj[0:rr].astype(BF16)
    rim_send[1] = adj[rr + s:].astype(BF16)
    before = lax.rem(b + last, last + 1)
    after = lax.rem(b + 1, last + 1)
    rims = [
        remote(rim_send.at[0], rim_recv.at[0], rim_ssem.at[0], rim_rsem.at[0],
               lat=lax.div(before, L), lon=lax.rem(before, L)),
        remote(rim_send.at[1], rim_recv.at[1], rim_ssem.at[1], rim_rsem.at[1],
               lat=lax.div(after, L), lon=lax.rem(after, L)),
    ]
    for copy in rims:
        copy.start()

    def return_fields():
        for copy in rims:
            copy.wait()
        from_next = jnp.where(b == last, 0.0, rim_recv[0].astype(F32))
        from_prev = jnp.where(b == 0, 0.0, rim_recv[1].astype(F32))
        adj[rr:2 * rr] += from_prev
        adj[s:s + rr] += from_next
        fg_band[...] = (
            bgrad[...].astype(F32).reshape(s, NL, C) + adj[rr:rr + s]
        ).astype(BF16)
        return send_tiles(fg_band, field_grad, fg_send, fg_recv)

    for h in groups:
        more = h + 1 < len(groups)
        if more:
            after_core(io_core, io_s0, io_g, io_c, h + 1)
            after_core(conv_core, conv_s0, conv_g, conv_c, h + 1)
        finish_stage(io_1[h])
        if more:
            io_1[h + 1] = stage_start("ens", io_s0, io_r1, h + 1, 0)
        stage_sum("ens", io_s0, io_r1, io_s1, h)
        io_2[h] = stage_start("lat", io_s1, io_r2, h, 2)
        finish_stage(conv_1[h])
        if more:
            conv_1[h + 1] = stage_start("lat", conv_s0, conv_r1, h + 1, 1)
        stage_sum("lat", conv_s0, conv_r1, conv_s1, h)
        conv_2[h] = stage_start("ens", conv_s1, conv_r2, h, 3)
        if h == 0:
            sends += return_fields()
        finish_stage(io_2[h])
        stage_sum("lat", io_s1, io_r2, io_s2, h)
        io_3[h] = lon_start(io_s2, io_r3, h, 0)
        finish_stage(conv_2[h])
        stage_sum("ens", conv_s1, conv_r2, conv_s2, h)
        conv_3[h] = lon_start(conv_s2, conv_r3, h, 1)
    await_tiles(block_out, bo_send, bo_recv)
    await_tiles(field_grad, fg_send, fg_recv)
    for h in groups:
        lon_sum(io_s2, io_r3, io_out, h, io_3[h])
        lon_sum(conv_s2, conv_r3, conv_out, h, conv_3[h])
    for copy in sends:
        copy.wait_send()


def finish(rows, factor, bo, fg, conv, io, block_out, field_grad, conv_grad, in_grad, out_grad):
    block_out[...] = bo[...]
    field_grad[...] = fg[...]
    conv_grad[...] = conv[...] * factor
    in_grad[...] = io[:rows] * factor
    out_grad[...] = io[rows:] * factor


def shards(fields, filter_basis, lon_offsets, conv_weight, weight_in, weight_out, cotangent):
    g = Plan(fields, filter_basis, weight_in)
    C, H, K, L, s = g.embed, g.hidden, g.basis, g.lon, g.band
    vmem, dma = pltpu.VMEM, pltpu.SemaphoreType.DMA
    rc, rio, half = g.conv_rows, 2 * g.in_rows, g.half
    peers = max(g.rows, g.members, 2) - 1

    def slots(n):
        return max(n - 1, 1)

    cuts = len(g.groups)
    after_ens, after_lat = half // g.members, half // g.rows
    scratch = [
        vmem(filter_basis.shape, BF16), vmem((g.span, s, g.taps), jnp.int32),
        vmem((s, (K + 1) * g.taps, g.span * g.nlon), F32), vmem((K * C, C), BF16), vmem((C, H), BF16), vmem((H, C), BF16),
        vmem((s + 2 * g.reach, g.nlon, C), BF16), vmem((s, g.nlon, C), BF16),
        vmem((s, K * g.nlon, g.span * g.nlon), BF16), vmem((g.cells, K * C), BF16),
        vmem((g.cells, C), BF16), vmem((g.cells, H), BF16), vmem((g.cells, H), BF16),
        vmem((g.cells, C), BF16), vmem((g.cells, K * C), BF16),
        vmem((s + 2 * g.reach, g.nlon, C), F32),
        vmem((s, g.nlon, C), BF16), vmem((s, g.nlon, C), BF16),
        vmem((2, g.reach, g.nlon, C), BF16), vmem((2, g.reach, g.nlon, C), BF16),
        vmem((g.cores, half, rc, C), BF16), vmem((g.cores, half, rio, C), BF16),
        vmem((half, rc, C), BF16), vmem((half, rio, C), BF16),
        vmem((half, rc, C), BF16), vmem((half, rio, C), BF16),
        vmem((slots(g.rows), after_lat, rc, C), BF16),
        vmem((slots(g.members), after_ens, rio, C), BF16),
        vmem((after_lat, rc, C), BF16), vmem((after_ens, rio, C), BF16),
        vmem((slots(g.members), L, rc, C), BF16), vmem((slots(g.rows), L, rio, C), BF16),
        vmem((L, rc, C), BF16), vmem((L, rio, C), BF16),
        vmem((slots(L), rc, C), BF16), vmem((slots(L), rio, C), BF16),
        dma((7,)), dma((slots(L), 3)), dma((slots(L), 3)), dma((4,)),
        dma((slots(L),)), dma((slots(L),)), dma((slots(L),)), dma((slots(L),)),
        dma((slots(L),)), dma((slots(L),)), dma((2,)), dma((2,)),
        dma((2, cuts)), dma((2, cuts)), dma((4, cuts, peers)), dma((4, cuts, peers)),
        dma((2, cuts, slots(L))), dma((2, cuts, slots(L))),
    ]
    in_vmem = pl.BlockSpec(memory_space=pltpu.VMEM)
    anywhere = pl.BlockSpec(memory_space=pl.ANY)
    block_out, field_grad, conv_sum, io_sum = pl.pallas_call(
        functools.partial(kernel, g),
        out_shape=(
            jax.ShapeDtypeStruct(fields.shape, BF16),
            jax.ShapeDtypeStruct(fields.shape, BF16),
            jax.ShapeDtypeStruct((rc, C), F32),
            jax.ShapeDtypeStruct((rio, C), F32),
        ),
        in_specs=[anywhere] * 7,
        out_specs=(in_vmem,) * 4,
        scratch_shapes=scratch,
        compiler_params=pltpu.CompilerParams(
            collective_id=0, has_side_effects=True, vmem_limit_bytes=56 * 1024 * 1024),
        cost_estimate=pl.CostEstimate(
            flops=24 * g.cells * C * H, bytes_accessed=16 * C * H, transcendentals=2 * g.cells * H),
    )(filter_basis, lon_offsets.transpose(1, 0, 2), fields, cotangent, conv_weight, weight_in, weight_out)

    factor = 1.0 / math.sqrt(g.ens * g.lat * L * g.cells)
    rows = g.in_rows
    if g.members == g.ens:
        outs = pl.pallas_call(
            functools.partial(finish, rows, factor),
            out_shape=(
                jax.ShapeDtypeStruct(fields.shape, BF16),
                jax.ShapeDtypeStruct(fields.shape, BF16),
                jax.ShapeDtypeStruct((rc, C), F32),
                jax.ShapeDtypeStruct((rows, C), F32),
                jax.ShapeDtypeStruct((rows, C), F32),
            ),
            in_specs=[in_vmem] * 4,
            out_specs=(in_vmem,) * 5,
        )(block_out, field_grad, conv_sum, io_sum)
        return outs[:3] + (outs[3].T, outs[4])
    conv_sum, in_sum, out_sum = (
        lax.psum_scatter(part.astype(BF16), "ens", scatter_dimension=0, tiled=True).astype(F32)
        for part in (conv_sum, io_sum[:rows], io_sum[rows:])
    )
    return (block_out, field_grad, conv_sum * factor, in_sum.T * factor, out_sum * factor)


def solution(mesh):
    tiles = P("ens", "lat", "lon", None)
    bands = ("lat", "lon")
    blocks = ("lat", "lon", "ens")
    return jax.shard_map(
        shards,
        mesh=mesh,
        in_specs=(tiles, P(bands, None, None, None), P(bands, None, None), P(), P(), P(), tiles),
        out_specs=(tiles, tiles, P(blocks, None), P(None, blocks), P(blocks, None)),
        check_vma=False,
    )
```

```python
import functools
import math

import jax
import jax.numpy as jnp
from jax import lax
from jax.experimental import pallas as pl
from jax.experimental.pallas import tpu as pltpu
from jax.sharding import PartitionSpec as P

HALF_ROOT = 0.7071067811865476
GAUSS_NORM = 0.3989422804014327
MESH = pl.DeviceIdType.MESH
F32 = jnp.float32
BF16 = jnp.bfloat16


def mm(left, right, contract):
    return lax.dot_general(left, right, ((contract[:1], contract[1:]), ((), ())),
                           preferred_element_type=F32)


class Plan:
    def __init__(self, fields, filter_basis, weight_in):
        self.lat, self.lon = lax.axis_size("lat"), lax.axis_size("lon")
        self.ens = lax.axis_size("ens")
        _, self.tile, self.width, self.embed = fields.shape
        self.band, self.span, self.basis, self.taps = filter_basis.shape
        self.hidden = weight_in.shape[1]
        self.reach = self.span // 2
        self.nlon = self.lon * self.width
        self.cells = self.band * self.nlon
        self.cores = 2 if self.lat % 2 == 0 else 1
        self.rows = self.lat // self.cores
        self.members = 1
        for members in (self.ens, 1):
            blocks = self.lat * self.lon * members
            conv_rows = self.basis * self.embed // blocks
            in_rows = self.hidden // blocks
            if conv_rows % 16 == 0 and in_rows % 8 == 0 and self.embed % conv_rows == 0:
                self.members = members
                break
        self.blocks = self.lat * self.lon * self.members
        self.conv_rows = self.basis * self.embed // self.blocks
        self.in_rows = self.hidden // self.blocks
        self.half = self.blocks // self.cores
        width = 256
        self.groups = [(c, min(width, self.embed - c)) for c in range(0, self.embed, width)]


def kernel(
    g, basis_hbm, offsets_hbm, fields, cot, conv_hbm, in_hbm, out_hbm,
    block_out, field_grad, conv_out, io_out,
    basis_ref, offsets_ref, taps_ref, conv_w, w_in, w_out, win, cot_band, matrix, spread, blended, hidden, slope, pgrad, bgrad,
    sgrad, adj, bo_band, fg_band, rim_send, rim_recv,
    conv_g, io_g, conv_c, io_c, conv_s0, io_s0, conv_r1, io_r1, conv_s1, io_s1,
    conv_r2, io_r2, conv_s2, io_s2, conv_r3, io_r3,
    local_sem, gather_send, gather_recv, edge_sem, cot_send, cot_recv,
    bo_send, bo_recv, fg_send, fg_recv, rim_ssem, rim_rsem,
    core_send, core_recv, st_send, st_recv, lon_send, lon_recv,
):
    a, j, e = lax.axis_index("lat"), lax.axis_index("lon"), lax.axis_index("ens")
    L, s, W, T, C = g.lon, g.band, g.width, g.tile, g.embed
    rr = g.reach
    core, y = lax.rem(a, g.cores), lax.div(a, g.cores)
    b = a * L + j
    last = g.lat * L - 1

    def remote(src, dst, ssem, rsem, **device):
        return pltpu.make_async_remote_copy(
            src_ref=src, dst_ref=dst, send_sem=ssem, recv_sem=rsem,
            device_id=device, device_id_type=MESH)

    def columns(index):
        return pl.ds(pl.multiple_of(index * W, W), W)

    weights = [
        pltpu.make_async_copy(src, dst, local_sem.at[i])
        for i, (src, dst) in enumerate(((conv_hbm, conv_w), (in_hbm, w_in), (out_hbm, w_out)))
    ]
    own_field = pltpu.make_async_copy(
        fields.at[0, pl.ds(j * s, s)], win.at[pl.ds(rr, s), columns(j)], local_sem.at[3])
    own_cot = pltpu.make_async_copy(
        cot.at[0, pl.ds(j * s, s)], cot_band.at[:, columns(j)], local_sem.at[4])
    basis_copy = pltpu.make_async_copy(basis_hbm, basis_ref, local_sem.at[5])
    offsets_copy = pltpu.make_async_copy(offsets_hbm, offsets_ref, local_sem.at[6])
    basis_copy.start()
    offsets_copy.start()
    own_field.start()
    own_cot.start()

    barrier = pltpu.get_barrier_semaphore()
    count = 0
    for step in (1, g.lat - 1):
        for q in range(L):
            pl.semaphore_signal(barrier, inc=1, device_id_type=MESH,
                                device_id={"lat": lax.rem(a + step, g.lat), "lon": q})
            count += 1
    for d in range(1, L):
        pl.semaphore_signal(barrier, inc=1, device_id_type=MESH,
                            device_id={"lon": lax.rem(j + d, L)})
        count += 1
    for d in range(1, g.rows):
        pl.semaphore_signal(barrier, inc=1, device_id_type=MESH,
                            device_id={"lat": lax.rem(y + d, g.rows) * g.cores + core})
        count += 1
    for d in range(1, g.members):
        pl.semaphore_signal(barrier, inc=1, device_id_type=MESH,
                            device_id={"ens": lax.rem(e + d, g.members)})
        count += 1
    pl.semaphore_wait(barrier, count)

    def low_src(p):
        return fields.at[0, pl.ds(lax.rem(p * s - rr + T, T), rr)]

    def high_src(p):
        return fields.at[0, pl.ds(lax.rem(p * s + s, T), rr)]

    low_rows, mid_rows, high_rows = pl.ds(0, rr), pl.ds(rr, s), pl.ds(rr + s, rr)

    def up(p):
        return lax.rem(a + (p == 0).astype(jnp.int32), g.lat)

    def down(p):
        return lax.rem(a + g.lat - (p == L - 1).astype(jnp.int32), g.lat)

    sends = []
    for d in range(1, L):
        p = lax.rem(j + d, L)
        triple = (
            (fields.at[0, pl.ds(p * s, s)], mid_rows, a),
            (low_src(p), low_rows, up(p)),
            (high_src(p), high_rows, down(p)),
        )
        for i, (src, rows, row) in enumerate(triple):
            copy = remote(src, win.at[rows, columns(j)], gather_send.at[d - 1, i],
                          gather_recv.at[d - 1, i], lat=row, lon=p)
            copy.start()
            sends.append(copy)
    low_local = pltpu.make_async_copy(low_src(j), win.at[low_rows, columns(j)], edge_sem.at[0])
    low_remote = remote(low_src(j), win.at[low_rows, columns(j)], edge_sem.at[2],
                        edge_sem.at[0], lat=lax.rem(a + 1, g.lat))
    high_local = pltpu.make_async_copy(high_src(j), win.at[high_rows, columns(j)], edge_sem.at[1])
    high_remote = remote(high_src(j), win.at[high_rows, columns(j)], edge_sem.at[3],
                         edge_sem.at[1], lat=lax.rem(a + g.lat - 1, g.lat))

    @pl.when(j == 0)
    def _():
        low_remote.start()

    @pl.when(j != 0)
    def _():
        low_local.start()

    @pl.when(j == L - 1)
    def _():
        high_remote.start()

    @pl.when(j != L - 1)
    def _():
        high_local.start()

    for copy in weights:
        copy.start()

    NL, K, TAPS = g.nlon, g.basis, g.taps
    wide = g.span * NL
    step_rows = 16
    steps = NL // step_rows
    places = lax.broadcasted_iota(jnp.int32, (step_rows, wide), 1)
    lines = lax.broadcasted_iota(jnp.int32, (step_rows, wide), 0)

    def build(i, _):
        r, n0 = lax.div(i, steps), lax.rem(i, steps) * step_rows
        gap = lax.rem(lax.rem(places, NL) - lines - n0 + (NL + NL // 2), NL) - NL // 2
        gap = gap.astype(F32)
        sums = [jnp.zeros((step_rows, wide), F32) for _ in range(K)]
        for t in range(TAPS):
            hit = gap == taps_ref[r, pl.ds(t, 1), :]
            for k in range(K):
                value = taps_ref[r, pl.ds(TAPS * (k + 1) + t, 1), :]
                sums[k] = jnp.where(hit, value, sums[k])
        for k in range(K):
            start = pl.multiple_of(k * NL + n0, step_rows)
            matrix[r, pl.ds(start, step_rows), :] = sums[k].astype(BF16)
        return 0

    ones = (lax.broadcasted_iota(jnp.int32, (g.span, wide), 1) // NL
            == lax.broadcasted_iota(jnp.int32, (g.span, wide), 0)).astype(BF16)
    basis_copy.wait()
    offsets_copy.wait()
    for r in range(s):
        taps_ref[r, 0:TAPS] = mm(offsets_ref[:, r, :].astype(F32).astype(BF16), ones, (0, 0))
        for k in range(K):
            taps_ref[r, TAPS * (k + 1):TAPS * (k + 2)] = mm(basis_ref[r, :, k, :], ones, (0, 0))
    lax.fori_loop(0, s * steps, build, 0)

    own_field.wait()
    for d in range(1, L):
        source = lax.rem(j - d + L, L)
        for i, rows in enumerate((mid_rows, low_rows, high_rows)):
            landed = win.at[rows, columns(source)]
            remote(landed, landed, gather_send.at[d - 1, i], gather_recv.at[d - 1, i],
                   lon=source).wait_recv()

    @pl.when(j == 0)
    def _():
        low_remote.wait()

    @pl.when(j != 0)
    def _():
        low_local.wait()

    @pl.when(j == L - 1)
    def _():
        high_remote.wait()

    @pl.when(j != L - 1)
    def _():
        high_local.wait()

    for d in range(1, L):
        p = lax.rem(j + d, L)
        copy = remote(cot.at[0, pl.ds(p * s, s)], cot_band.at[:, columns(j)],
                      cot_send.at[d - 1], cot_recv.at[d - 1], lon=p)
        copy.start()
        sends.append(copy)

    @pl.when(b == 0)
    def _():
        win[0:rr] = jnp.zeros((rr, NL, C), BF16)

    @pl.when(b == last)
    def _():
        win[rr + s:] = jnp.zeros((rr, NL, C), BF16)

    for r in range(s):
        window = win[r:r + g.span].reshape(wide, C)
        part = mm(matrix[r], window, (1, 0)).astype(BF16)
        for k in range(K):
            spread[r * NL:(r + 1) * NL, k * C:(k + 1) * C] = part[k * NL:(k + 1) * NL]
    weights[0].wait()
    blended[...] = (
        win[rr:rr + s].reshape(g.cells, C).astype(F32) + mm(spread[...], conv_w[...], (1, 0))
    ).astype(BF16)

    weights[1].wait()
    weights[2].wait()
    lanes = 256 if g.hidden % 256 == 0 else g.hidden

    def unit_cols(i):
        return pl.ds(pl.multiple_of(i * lanes, lanes), lanes)

    def units(i, _):
        cols = unit_cols(i)
        pre = mm(blended[...], w_in[:, cols], (1, 0))
        cdf = 0.5 * (1.0 + lax.erf(pre * HALF_ROOT))
        hidden[:, cols] = (pre * cdf).astype(BF16)
        slope[:, cols] = cdf + pre * jnp.exp(-0.5 * pre * pre) * GAUSS_NORM
        return 0

    def unit_grads(i, _):
        cols = unit_cols(i)
        hgrad = mm(cot_band[...].reshape(g.cells, C), w_out[cols, :], (1, 1))
        pgrad[:, cols] = (hgrad * slope[:, cols]).astype(BF16)
        return 0

    lax.fori_loop(0, g.hidden // lanes, units, 0)
    bo_band[...] = (
        blended[...].astype(F32) + mm(hidden[...], w_out[...], (1, 0))
    ).astype(BF16).reshape(s, NL, C)
    own_cot.wait()
    for d in range(1, L):
        source = lax.rem(j - d + L, L)
        landed = cot_band.at[:, columns(source)]
        remote(landed, landed, cot_send.at[d - 1], cot_recv.at[d - 1], lon=source).wait_recv()
    lax.fori_loop(0, g.hidden // lanes, unit_grads, 0)

    def send_tiles(band, out, ssem, rsem):
        copies = []
        for d in range(1, L):
            p = lax.rem(j + d, L)
            copy = remote(band.at[:, columns(p)], out.at[0, pl.ds(j * s, s)],
                          ssem.at[d - 1], rsem.at[d - 1], lon=p)
            copy.start()
            copies.append(copy)
        out[0, pl.ds(j * s, s)] = band[:, columns(j), :]
        return copies

    def await_tiles(out, ssem, rsem):
        for d in range(1, L):
            source = lax.rem(j - d + L, L)
            landed = out.at[0, pl.ds(source * s, s)]
            remote(landed, landed, ssem.at[d - 1], rsem.at[d - 1], lon=source).wait_recv()

    E, Y, half = g.members, g.rows, g.half
    ri, rc = g.in_rows, g.conv_rows
    groups = range(len(g.groups))

    def place(index, order):
        member = lax.rem(index, E)
        column = lax.rem(lax.div(index, E), L)
        row = lax.div(index, E * L)
        row_core, row_y = lax.rem(row, g.cores), lax.div(row, g.cores)
        outer = member * Y + row_y if order == "ens" else row_y * E + member
        return row_core, outer * L + column

    def cut(h):
        return pl.ds(*g.groups[h])

    def add(blocks):
        if len(blocks) == 2:
            return blocks[0] + blocks[1]
        return sum((block.astype(F32) for block in blocks[1:]), blocks[0].astype(F32)).astype(BF16)

    def io_blocks(h):
        first, count = g.groups[h]

        def one(i, _):
            cols = pl.ds(pl.multiple_of(i * C, 128), C)
            left = mm(pgrad[:, cols], blended[:, cut(h)], (0, 0))
            tangent = cot_band[:, :, first:first + count].reshape(g.cells, count)
            right = mm(hidden[:, cols], tangent, (0, 0))
            for c in range(C // ri):
                where, flat = place(i * (C // ri) + c, "ens")
                both = jnp.concatenate(
                    [left[c * ri:(c + 1) * ri], right[c * ri:(c + 1) * ri]], 0)
                io_g[where, flat, :, cut(h)] = both.astype(BF16)
            return 0

        lax.fori_loop(0, g.hidden // C, one, 0)

    def conv_blocks(h):
        def one(i, _):
            cols = pl.ds(pl.multiple_of(i * C, 128), C)
            product = mm(spread[:, cols], bgrad[:, cut(h)], (0, 0))
            for c in range(C // rc):
                where, flat = place(i * (C // rc) + c, "lat")
                conv_g[where, flat, :, cut(h)] = product[c * rc:(c + 1) * rc].astype(BF16)
            return 0

        lax.fori_loop(0, K, one, 0)

    def core_copies(src, dst, index):
        return [
            remote(src.at[1 - core, :, :, cut(h)], dst.at[:, :, cut(h)],
                   core_send.at[index, h], core_recv.at[index, h],
                   lat=y * g.cores + 1 - core)
            for h in groups
        ]

    def core_sum(total, own, other, h):
        def one(i, _):
            blocks = [own[core, i, :, cut(h)]]
            if g.cores > 1:
                blocks.append(other[i, :, cut(h)])
            total[i, :, cut(h)] = add(blocks)
            return 0
        lax.fori_loop(0, half, one, 0)

    def stage(axis):
        if axis == "ens":
            return E, e, [({"ens": lax.rem(e + d, E)}, lax.rem(e + d, E)) for d in range(1, E)]
        turns = [lax.rem(y + d, Y) for d in range(1, Y)]
        return Y, y, [({"lat": p * g.cores + core}, p) for p in turns]

    def stage_start(axis, src, dst, h, sem_row):
        _, _, peers = stage(axis)
        m = dst.shape[1]
        copies = []
        for d, (device, p) in enumerate(peers):
            copy = remote(src.at[pl.ds(p * m, m), :, cut(h)], dst.at[d, :, :, cut(h)],
                          st_send.at[sem_row, h, d], st_recv.at[sem_row, h, d], **device)
            copy.start()
            copies.append(copy)
        return copies

    def stage_sum(axis, src, dst, total, h):
        n, me, _ = stage(axis)
        m = dst.shape[1]

        def one(i, _):
            total[i, :, cut(h)] = add(
                [src[me * m + i, :, cut(h)]] + [dst[d, i, :, cut(h)] for d in range(n - 1)])
            return 0

        lax.fori_loop(0, m, one, 0)

    def lon_start(src, dst, h, sem_row):
        copies = []
        for d in range(1, L):
            p = lax.rem(j + d, L)
            copy = remote(src.at[p, :, cut(h)], dst.at[d - 1, :, cut(h)],
                          lon_send.at[sem_row, h, d - 1], lon_recv.at[sem_row, h, d - 1], lon=p)
            copy.start()
            copies.append(copy)
        return copies

    def lon_sum(src, dst, total, h, copies):
        block = src[j, :, cut(h)].astype(F32)
        for d, copy in enumerate(copies):
            copy.wait()
            block = block + dst[d, :, cut(h)].astype(F32)
        total[:, cut(h)] = block

    io_core = core_copies(io_g, io_c, 0)
    conv_core = core_copies(conv_g, conv_c, 1)
    io_1, conv_1, io_2, conv_2, io_3, conv_3 = ([None for _ in groups] for _ in range(6))

    def to_core(copies, h):
        if g.cores > 1:
            copies[h].start()

    def after_core(copies, total, own, other, h):
        if g.cores > 1:
            copies[h].wait()
        core_sum(total, own, other, h)

    def finish_stage(copies):
        for copy in copies:
            copy.wait()

    io_blocks(0)
    to_core(io_core, 0)
    bgrad[...] = (
        cot_band[...].reshape(g.cells, C).astype(F32) + mm(pgrad[...], w_in[...], (1, 1))
    ).astype(BF16)
    after_core(io_core, io_s0, io_g, io_c, 0)
    io_1[0] = stage_start("ens", io_s0, io_r1, 0, 0)
    conv_blocks(0)
    to_core(conv_core, 0)
    for h in groups[1:]:
        io_blocks(h)
        to_core(io_core, h)
    after_core(conv_core, conv_s0, conv_g, conv_c, 0)
    conv_1[0] = stage_start("lat", conv_s0, conv_r1, 0, 1)
    sends += send_tiles(bo_band, block_out, bo_send, bo_recv)
    for h in groups[1:]:
        conv_blocks(h)
        to_core(conv_core, h)

    sgrad[...] = mm(bgrad[...], conv_w[...], (1, 1)).astype(BF16)
    for r in range(s):
        grad = jnp.concatenate(
            [sgrad[r * NL:(r + 1) * NL, k * C:(k + 1) * C] for k in range(K)], 0)
        part = mm(matrix[r], grad, (0, 0)).reshape(g.span, NL, C)
        if r == 0:
            adj[0:g.span] = part
            adj[g.span:] = jnp.zeros((s - 1, NL, C), F32)
        else:
            adj[r:r + g.span] += part

    rim_send[0] = adj[0:rr].astype(BF16)
    rim_send[1] = adj[rr + s:].astype(BF16)
    before = lax.rem(b + last, last + 1)
    after = lax.rem(b + 1, last + 1)
    rims = [
        remote(rim_send.at[0], rim_recv.at[0], rim_ssem.at[0], rim_rsem.at[0],
               lat=lax.div(before, L), lon=lax.rem(before, L)),
        remote(rim_send.at[1], rim_recv.at[1], rim_ssem.at[1], rim_rsem.at[1],
               lat=lax.div(after, L), lon=lax.rem(after, L)),
    ]
    for copy in rims:
        copy.start()

    def return_fields():
        for copy in rims:
            copy.wait()
        from_next = jnp.where(b == last, 0.0, rim_recv[0].astype(F32))
        from_prev = jnp.where(b == 0, 0.0, rim_recv[1].astype(F32))
        adj[rr:2 * rr] += from_prev
        adj[s:s + rr] += from_next
        fg_band[...] = (
            bgrad[...].astype(F32).reshape(s, NL, C) + adj[rr:rr + s]
        ).astype(BF16)
        return send_tiles(fg_band, field_grad, fg_send, fg_recv)

    for h in groups:
        more = h + 1 < len(groups)
        if more:
            after_core(io_core, io_s0, io_g, io_c, h + 1)
            after_core(conv_core, conv_s0, conv_g, conv_c, h + 1)
        finish_stage(io_1[h])
        if more:
            io_1[h + 1] = stage_start("ens", io_s0, io_r1, h + 1, 0)
        stage_sum("ens", io_s0, io_r1, io_s1, h)
        io_2[h] = stage_start("lat", io_s1, io_r2, h, 2)
        finish_stage(conv_1[h])
        if more:
            conv_1[h + 1] = stage_start("lat", conv_s0, conv_r1, h + 1, 1)
        stage_sum("lat", conv_s0, conv_r1, conv_s1, h)
        conv_2[h] = stage_start("ens", conv_s1, conv_r2, h, 3)
        if h == 0:
            sends += return_fields()
        finish_stage(io_2[h])
        stage_sum("lat", io_s1, io_r2, io_s2, h)
        io_3[h] = lon_start(io_s2, io_r3, h, 0)
        finish_stage(conv_2[h])
        stage_sum("ens", conv_s1, conv_r2, conv_s2, h)
        conv_3[h] = lon_start(conv_s2, conv_r3, h, 1)
    await_tiles(block_out, bo_send, bo_recv)
    await_tiles(field_grad, fg_send, fg_recv)
    for h in groups:
        lon_sum(io_s2, io_r3, io_out, h, io_3[h])
        lon_sum(conv_s2, conv_r3, conv_out, h, conv_3[h])
    for copy in sends:
        copy.wait_send()


def finish(rows, factor, bo, fg, conv, io, block_out, field_grad, conv_grad, in_grad, out_grad):
    block_out[...] = bo[...]
    field_grad[...] = fg[...]
    conv_grad[...] = conv[...] * factor
    in_grad[...] = io[:rows] * factor
    out_grad[...] = io[rows:] * factor


def shards(fields, filter_basis, lon_offsets, conv_weight, weight_in, weight_out, cotangent):
    g = Plan(fields, filter_basis, weight_in)
    C, H, K, L, s = g.embed, g.hidden, g.basis, g.lon, g.band
    vmem, dma = pltpu.VMEM, pltpu.SemaphoreType.DMA
    rc, rio, half = g.conv_rows, 2 * g.in_rows, g.half
    peers = max(g.rows, g.members, 2) - 1

    def slots(n):
        return max(n - 1, 1)

    cuts = len(g.groups)
    after_ens, after_lat = half // g.members, half // g.rows
    scratch = [
        vmem(filter_basis.shape, BF16), vmem((g.span, s, g.taps), jnp.int32),
        vmem((s, (K + 1) * g.taps, g.span * g.nlon), F32), vmem((K * C, C), BF16), vmem((C, H), BF16), vmem((H, C), BF16),
        vmem((s + 2 * g.reach, g.nlon, C), BF16), vmem((s, g.nlon, C), BF16),
        vmem((s, K * g.nlon, g.span * g.nlon), BF16), vmem((g.cells, K * C), BF16),
        vmem((g.cells, C), BF16), vmem((g.cells, H), BF16), vmem((g.cells, H), F32),
        vmem((g.cells, H), BF16),
        vmem((g.cells, C), BF16), vmem((g.cells, K * C), BF16),
        vmem((s + 2 * g.reach, g.nlon, C), F32),
        vmem((s, g.nlon, C), BF16), vmem((s, g.nlon, C), BF16),
        vmem((2, g.reach, g.nlon, C), BF16), vmem((2, g.reach, g.nlon, C), BF16),
        vmem((g.cores, half, rc, C), BF16), vmem((g.cores, half, rio, C), BF16),
        vmem((half, rc, C), BF16), vmem((half, rio, C), BF16),
        vmem((half, rc, C), BF16), vmem((half, rio, C), BF16),
        vmem((slots(g.rows), after_lat, rc, C), BF16),
        vmem((slots(g.members), after_ens, rio, C), BF16),
        vmem((after_lat, rc, C), BF16), vmem((after_ens, rio, C), BF16),
        vmem((slots(g.members), L, rc, C), BF16), vmem((slots(g.rows), L, rio, C), BF16),
        vmem((L, rc, C), BF16), vmem((L, rio, C), BF16),
        vmem((slots(L), rc, C), BF16), vmem((slots(L), rio, C), BF16),
        dma((7,)), dma((slots(L), 3)), dma((slots(L), 3)), dma((4,)),
        dma((slots(L),)), dma((slots(L),)), dma((slots(L),)), dma((slots(L),)),
        dma((slots(L),)), dma((slots(L),)), dma((2,)), dma((2,)),
        dma((2, cuts)), dma((2, cuts)), dma((4, cuts, peers)), dma((4, cuts, peers)),
        dma((2, cuts, slots(L))), dma((2, cuts, slots(L))),
    ]
    in_vmem = pl.BlockSpec(memory_space=pltpu.VMEM)
    anywhere = pl.BlockSpec(memory_space=pl.ANY)
    block_out, field_grad, conv_sum, io_sum = pl.pallas_call(
        functools.partial(kernel, g),
        out_shape=(
            jax.ShapeDtypeStruct(fields.shape, BF16),
            jax.ShapeDtypeStruct(fields.shape, BF16),
            jax.ShapeDtypeStruct((rc, C), F32),
            jax.ShapeDtypeStruct((rio, C), F32),
        ),
        in_specs=[anywhere] * 7,
        out_specs=(in_vmem,) * 4,
        scratch_shapes=scratch,
        compiler_params=pltpu.CompilerParams(
            collective_id=0, has_side_effects=True, vmem_limit_bytes=56 * 1024 * 1024),
        cost_estimate=pl.CostEstimate(
            flops=24 * g.cells * C * H, bytes_accessed=16 * C * H, transcendentals=2 * g.cells * H),
    )(filter_basis, lon_offsets.transpose(1, 0, 2), fields, cotangent, conv_weight, weight_in, weight_out)

    factor = 1.0 / math.sqrt(g.ens * g.lat * L * g.cells)
    rows = g.in_rows
    if g.members == g.ens:
        outs = pl.pallas_call(
            functools.partial(finish, rows, factor),
            out_shape=(
                jax.ShapeDtypeStruct(fields.shape, BF16),
                jax.ShapeDtypeStruct(fields.shape, BF16),
                jax.ShapeDtypeStruct((rc, C), F32),
                jax.ShapeDtypeStruct((rows, C), F32),
                jax.ShapeDtypeStruct((rows, C), F32),
            ),
            in_specs=[in_vmem] * 4,
            out_specs=(in_vmem,) * 5,
        )(block_out, field_grad, conv_sum, io_sum)
        return outs[:3] + (outs[3].T, outs[4])
    conv_sum, in_sum, out_sum = (
        lax.psum_scatter(part.astype(BF16), "ens", scatter_dimension=0, tiled=True).astype(F32)
        for part in (conv_sum, io_sum[:rows], io_sum[rows:])
    )
    return (block_out, field_grad, conv_sum * factor, in_sum.T * factor, out_sum * factor)


def solution(mesh):
    tiles = P("ens", "lat", "lon", None)
    bands = ("lat", "lon")
    blocks = ("lat", "lon", "ens")
    return jax.shard_map(
        shards,
        mesh=mesh,
        in_specs=(tiles, P(bands, None, None, None), P(bands, None, None), P(), P(), P(), tiles),
        out_specs=(tiles, tiles, P(blocks, None), P(None, blocks), P(blocks, None)),
        check_vma=False,
    )
```
